256 devices in a mesh: slide: 32 (over x, y, core), tile: 8 (over z).
Axes of the slice: x: 4, y: 4, z: 8, core: 2. Of those that a mesh axis runs over, the one named last changes fastest.
Arguments:
- image: bfloat16 [32, 3, 64, 2048], P('slide', None, 'tile'), may hold values from -6 to 6
- stem_weight: bfloat16 [147, 64], replicated, may hold values from -0.5 to 0.5
- conv_weight: bfloat16 [576, 64], replicated, may hold values from -0.25 to 0.25
- expand_weight: bfloat16 [64, 256], replicated, may hold values from -0.75 to 0.75
- cotangent: bfloat16 [32, 32, 262144], P('slide', 'tile'), may hold values from -6 to 6
- tissue: int32 [32, 1, 4], P('slide'), may hold values 0 or 1
Outputs:
- stem_grad: bfloat16 [32, 32, 65536], P('slide', 'tile')
- stem_wgrad: float32 [147, 64], replicated
- conv_wgrad: float32 [576, 64], replicated
- expand_wgrad: float32 [64, 256], replicated
The draws below stay inside these ranges and needn't reach their ends.
All inputs are finite; a program needn't handle non-finite values. No bound on the sum of `tissue` on one device may be relied on, other than what follows from the above.
Results may differ from the reference program's by a relative error of at most 0.0055.
Values may be sent and summed in bfloat16 or wider, within the bound.
No kernel may reach another device: no remote copies, remote signals or barrier semaphores. Data moves between devices by JAX's collectives and lax.ppermute only.
A program may use at most 64 MiB of HBM per device.

```python
import math
import jax
import jax.numpy as jnp
from jax import lax

CH = 64
OUT_CH = 256
COLS = 1024
TILE = 256
SLIDES = 32
ROWS = 32
IN_ROWS = 64
IN_COLS = 2048


def set_ends(result, stream_key, low, largest):
    spot = [jax.random.randint(jax.random.fold_in(stream_key, axis), (), 0, length) for axis, length in enumerate(result.shape)]
    widest = result.shape.index(max(result.shape))
    next_to = spot[:widest] + [(spot[widest] + 1) % result.shape[widest]] + spot[widest + 1:]
    return result.at[tuple(spot)].set(low).at[tuple(next_to)].set(largest)


def levels(key, shape, cuts, low, top_value):
    def one(dim, parts):
        draws = jax.random.uniform(jax.random.fold_in(jax.random.fold_in(key, 6), dim), (parts,), jnp.float32, low / len(cuts), top_value / len(cuts))
        return jnp.repeat(jnp.exp(draws), shape[dim] // parts).reshape((-1,) + (1,) * (len(shape) - dim - 1))

    factor_of = one(*cuts[0])
    for cut in cuts[1:]:
        factor_of = factor_of * one(*cut)
    return factor_of


def gaussian(rng, shape, deviation, limit, shards=(), dtype=jnp.bfloat16):
    values = jax.random.normal(rng, shape, jnp.float32) * deviation
    if len(shards) > 0:
        values = levels(rng, shape, shards, -0.22, 0.18) * values
    return jnp.clip(values, min=-limit, max=limit).astype(dtype)


def setup_inputs(seed: int = 0) -> dict:
    streams_of = jax.random.split(jax.random.key(seed), 7)
    return {
        "image": gaussian(streams_of[0], (SLIDES, 3, IN_ROWS, IN_COLS), 1.0, 6.0, ((0, 32), (2, 8))),
        "stem_weight": gaussian(streams_of[1], (147, CH), 147 ** -0.5, 0.5),
        "conv_weight": gaussian(streams_of[2], (9 * CH, CH), (9 * CH) ** -0.5, 0.25),
        "expand_weight": gaussian(streams_of[3], (CH, OUT_CH), CH ** -0.5, 0.75),
        "cotangent": gaussian(streams_of[4], (SLIDES, ROWS, COLS * OUT_CH), 1.0, 6.0, ((0, 32), (1, 8))),
        "tissue": set_ends((jax.random.randint(streams_of[5], (SLIDES, 1, COLS // TILE), 0, 5) < 3).astype(jnp.int32), jax.random.fold_in(streams_of[5], 1), 0, 1),
    }


def silu_slope(value):
    sig = jax.nn.sigmoid(value)
    return sig * (1.0 + value * (1.0 - sig))

def stem_patches(padded, nrows, ncols):
    pieces = []
    for i in range(7):
        for j in range(7):
            pieces.append(lax.slice(padded, (0, i, j), (3, i + 2 * nrows - 1, j + 2 * ncols - 1), (1, 2, 2)))
    stacked = jnp.stack(pieces, 0)
    return jnp.transpose(stacked, (2, 3, 0, 1)).reshape(nrows * ncols, 147)

def one_slide(image, cotangent, tissue, stem_weight, conv_weight, expand_weight):
    channels = stem_weight.shape[1]
    padded = jnp.pad(image, ((0, 0), (3, 3), (3, 3)))
    patches = stem_patches(padded, ROWS, COLS)
    pre1 = jnp.dot(patches, stem_weight, preferred_element_type=jnp.float32)
    act1 = jax.nn.silu(pre1).astype(jnp.bfloat16).reshape(ROWS, COLS, channels)
    act1_pad = jnp.pad(act1, ((1, 1), (1, 1), (0, 0)))
    shifted = [act1_pad[i:i + ROWS, j:j + COLS].reshape(-1, channels) for i in range(3) for j in range(3)]
    pre2 = jnp.zeros((ROWS * COLS, channels), jnp.float32)
    for idx in range(9):
        pre2 = pre2 + jnp.dot(shifted[idx], conv_weight[idx * channels:(idx + 1) * channels], preferred_element_type=jnp.float32)
    act2 = jax.nn.silu(pre2).astype(jnp.bfloat16)
    column_mask = jnp.repeat(tissue[0], TILE).astype(jnp.bfloat16)
    masked = (cotangent.reshape(ROWS, COLS, OUT_CH) * column_mask[None, :, None]).reshape(-1, OUT_CH)
    expand_sum = lax.dot_general(act2, masked, (((0,), (0,)), ((), ())), preferred_element_type=jnp.float32)
    back2 = jnp.dot(masked, expand_weight.T, preferred_element_type=jnp.float32)
    grad2 = (back2 * silu_slope(pre2)).astype(jnp.bfloat16)
    conv_sum = jnp.concatenate([lax.dot_general(shifted[idx], grad2, (((0,), (0,)), ((), ())), preferred_element_type=jnp.float32) for idx in range(9)], 0)
    grad2_pad = jnp.pad(grad2.reshape(ROWS, COLS, channels), ((1, 1), (1, 1), (0, 0)))
    back1 = jnp.zeros((ROWS * COLS, channels), jnp.float32)
    for i in range(3):
        for j in range(3):
            idx = i * 3 + j
            window = grad2_pad[2 - i:2 - i + ROWS, 2 - j:2 - j + COLS].reshape(-1, channels)
            back1 = back1 + jnp.dot(window, conv_weight[idx * channels:(idx + 1) * channels].T, preferred_element_type=jnp.float32)
    stem_grad = (back1 * silu_slope(pre1)).astype(jnp.bfloat16)
    stem_sum = lax.dot_general(patches, stem_grad, (((0,), (0,)), ((), ())), preferred_element_type=jnp.float32)
    return (stem_grad.reshape(ROWS, COLS * channels), stem_sum, conv_sum, expand_sum)

def reference(image, stem_weight, conv_weight, expand_weight, cotangent, tissue):

    def step(carry, items):
        grad, stem_sum, conv_sum, expand_sum = one_slide(items[0], items[1], items[2], stem_weight, conv_weight, expand_weight)
        return ((carry[0] + stem_sum, carry[1] + conv_sum, carry[2] + expand_sum), grad)
    channels = stem_weight.shape[1]
    start = (jnp.zeros((147, channels), jnp.float32), jnp.zeros((9 * channels, channels), jnp.float32), jnp.zeros((channels, OUT_CH), jnp.float32))
    totals, grads = lax.scan(step, start, (image, cotangent, tissue))
    factor = 1.0 / math.sqrt(SLIDES * ROWS * COLS)
    return (grads, totals[0] * factor, totals[1] * factor, totals[2] * factor)
```

```python
import jax
import jax.numpy as jnp
from jax import lax
from jax.experimental import pallas as pl
from jax.experimental.layout import Layout, with_layout_constraint
from jax.experimental.pallas import tpu as pltpu
from jax.sharding import Mesh, PartitionSpec as P

F32 = jnp.float32
BF16 = jnp.bfloat16
VMEM_LIMIT = 56 * 1024 * 1024

ROW_OF = (1, 2, 3, 4, 0, 5)
SLOT_OF = (4, 0, 1, 2, 3, 5)
PAD = 8


def dot_t(left, right):
    return lax.dot_general(left, right, (((1,), (1,)), ((), ())), preferred_element_type=F32)


def dot_0(left, right):
    return lax.dot_general(left, right, (((0,), (0,)), ((), ())), preferred_element_type=F32)


def dot_n(left, right):
    return jnp.dot(left, right, preferred_element_type=F32)


def iota(shape, dim):
    return lax.broadcasted_iota(jnp.int32, shape, dim)


def lane_is_low(rows):
    return iota((rows, 128), 1) < 64


def stem_places(row, count, split):
    lane = iota((1, 512), 1)
    tap = lane // 64
    within = lane % 64
    colour = (within >= 18).astype(jnp.int32) + (within >= 36).astype(jnp.int32)
    line = within - 18 * colour - 2 * row
    valid = (tap >= 1) & (within < 54) & (line >= 0) & (line <= 6)
    entry = line * 21 + (tap - 1) * 3 + colour
    if split:
        entry = jnp.where(entry < 128, entry, entry + 64)
    entry = jnp.where(valid, entry, -1)
    return (iota((count, 512), 0) == entry).astype(F32).astype(BF16)


def prepare_kernel(tissue, cot, stem_t, conv_t, expand, cot_f, back2, w1, w2, w2b, order, wide):
    step = pl.program_id(0)

    @pl.when(step == 0)
    def _():
        m, k = iota((256, 256), 0), iota((256, 256), 1)
        source = (m % 32) * 8 + ((m // 32) % 2) * 4 + m // 64
        order[...] = (k == source).astype(F32).astype(BF16)
        wide[...] = jnp.zeros(wide.shape, BF16)
        for r in range(4):
            wide[r * 64 : (r + 1) * 64, r * 256 : (r + 1) * 256] = expand[...]
        stem = stem_t[...]
        for slot in range(6):
            w1[slot * 64 : (slot + 1) * 64, :] = dot_n(stem, stem_places(ROW_OF[slot], 256, False)).astype(BF16)
        blocks = [conv_t[:, n * 64 : (n + 1) * 64].astype(F32) for n in range(9)]
        none = jnp.zeros((64, 64), F32)

        def block(i, j):
            return blocks[3 * i + j] if 0 <= i <= 2 else none

        for j in range(3):
            for r in range(4):
                for t in range(3):
                    pair = [block(ROW_OF[2 * t + e] - r, j) for e in range(2)]
                    w2[r * 64 : (r + 1) * 64, j * 384 + t * 128 : j * 384 + (t + 1) * 128] = jnp.concatenate(pair, 1).astype(BF16)
            for slot in range(6):
                for t in range(2):
                    pair = [block(2 * t + e - ROW_OF[slot] + 2, j) for e in range(2)]
                    w2b[slot * 64 : (slot + 1) * 64, j * 256 + t * 128 : j * 256 + (t + 1) * 128] = jnp.concatenate(pair, 1).astype(BF16)

    for s in range(8):
        got = dot_n(order[...], cot[s * 256 : (s + 1) * 256, :]).astype(BF16)
        for n in range(8):
            cot_f[s * 32 : (s + 1) * 32, n * 128 : (n + 1) * 128] = got[n * 32 : (n + 1) * 32, :]
    keep = tissue[0, step].astype(F32)
    back2[...] = dot_t(cot_f[...], wide[...]) * keep


def forward_kernel(tissue, place, before, own, after, w1, w2, back2, z, act_sh, slope1, act2, grad2, edge, lines, cols, field):
    lines[54:64, :] = jnp.zeros((10, 2048), F32)
    for k in range(3):
        lines[18 * k : 18 * k + 5, :] = before[0, k, 3:8, :].astype(F32)
        lines[18 * k + 5 : 18 * k + 13, :] = own[0, k].astype(F32)
        lines[18 * k + 13 : 18 * k + 18, :] = after[0, k, 0:5, :].astype(F32)
    m, x = iota((128, 512), 0), iota((128, 512), 1)
    pick = (x == jnp.where(x < 256, 2 * m, 2 * m + 257)).astype(F32).astype(BF16)
    cols[0:PAD, :] = jnp.zeros((PAD, 128), F32)
    cols[PAD + 1024 :, :] = jnp.zeros((PAD, 128), F32)
    field[0:PAD, :] = jnp.zeros((PAD, 384), F32)
    field[PAD + 1024 :, :] = jnp.zeros((PAD, 384), F32)
    none = jnp.zeros((64, 256), BF16)
    for t in range(8):
        part = lines[:, t * 256 : (t + 1) * 256].astype(BF16)
        spread = jnp.concatenate([jnp.concatenate([part, none], 0), jnp.concatenate([none, part], 0)], 1)
        cols[PAD + t * 128 : PAD + (t + 1) * 128, :] = dot_t(pick, spread)
    above, below = place[0, 0].astype(F32), place[0, 1].astype(F32)
    ends = jnp.where(lane_is_low(1), above, below)
    for t in range(8):
        at = t * 128
        wins = [cols[PAD + at + s : PAD + at + s + 128, :].astype(BF16) for s in (-2, -1, 0, 1)]
        zt = jnp.concatenate(wins, 1)
        z[at : at + 128, :] = zt
        pre = dot_t(zt, w1[...])
        sig = 1.0 / (1.0 + jnp.exp(-pre))
        act = pre * sig
        field[PAD + at : PAD + at + 128, 0:256] = act[:, :256]
        field[PAD + at : PAD + at + 128, 256:384] = act[:, 256:] * ends
        slope1[at : at + 128, :] = (sig * (1.0 + pre * (1.0 - sig)))[:, :256]
    for t in range(8):
        at = t * 128
        wins = [field[PAD + at + j - 1 : PAD + at + j + 127, :].astype(BF16) for j in range(3)]
        sh = jnp.concatenate(wins, 1)
        act_sh[at : at + 128, :] = sh
        pre = dot_t(sh, w2[...])
        sig = 1.0 / (1.0 + jnp.exp(-pre))
        keep = tissue[0, t // 2].astype(F32)
        act2[at : at + 128, :] = (pre * sig * keep).astype(BF16)
        slope = sig * (1.0 + pre * (1.0 - sig))
        grad2[at : at + 128, :] = (back2[at : at + 128, :] * slope).astype(BF16)
    low = lane_is_low(512)
    a, b = grad2[0:512, 0:128].astype(F32), grad2[512:1024, 0:128].astype(F32)
    edge[0] = jnp.where(low, a, pltpu.roll(b, 64, 1)).astype(BF16)
    a, b = grad2[0:512, 128:256].astype(F32), grad2[512:1024, 128:256].astype(F32)
    edge[1] = jnp.where(low, pltpu.roll(a, 64, 1), b).astype(BF16)


def filters_kernel(act_sh, act2, grad2, cot_f, sums):
    prod = dot_0(grad2[...], act_sh[...])
    low = lane_is_low(64)
    halves = {}
    for i in range(3):
        for j in range(3):
            at_low, at_high = [], []
            for r in range(4):
                slot = SLOT_OF[r + i]
                col = j * 384 + (slot // 2) * 128
                tile = prod[r * 64 : (r + 1) * 64, col : col + 128]
                (at_high if slot % 2 else at_low).append(tile)
            halves[3 * i + j] = (sum(at_low[1:], at_low[0]), sum(at_high[1:], at_high[0]))
    for u in range(5):
        a, b = halves[2 * u]
        left = a + pltpu.roll(b, 64, 1)
        if u == 4:
            tile = jnp.where(low, left, 0.0)
        else:
            a, b = halves[2 * u + 1]
            tile = jnp.where(low, left, pltpu.roll(a, 64, 1) + b)
        sums[u * 64 : (u + 1) * 64, :] = tile
    total = None
    for t in range(2):
        pair = dot_0(act2[:, t * 128 : (t + 1) * 128], cot_f[:, t * 512 : (t + 1) * 512])
        part = pair[0:64, 0:256] + pair[64:128, 256:512]
        total = part if total is None else total + part
    sums[320:384, :] = total[:, 0:128]
    sums[384:448, :] = total[:, 128:256]


def backward_kernel(z, slope1, grad2, halo_a, halo_b, w2b, sums, out, totals, wide, mixed):
    low = lane_is_low(512)
    a, b = halo_a[...].astype(F32), halo_b[...].astype(F32)
    ends = [jnp.where(low, a, pltpu.roll(b, 64, 1)).astype(BF16), jnp.where(low, pltpu.roll(a, 64, 1), b).astype(BF16)]
    wide[0:PAD, :] = jnp.zeros((PAD, 768), F32)
    wide[PAD + 1024 :, :] = jnp.zeros((PAD, 768), F32)
    for t in range(8):
        at = t * 128
        end = ends[t // 4][(t % 4) * 128 : (t % 4 + 1) * 128, :]
        left = jnp.concatenate([grad2[at : at + 128, :], end], 1)
        wide[PAD + at : PAD + at + 128, :] = dot_n(left, w2b[...])
    for t in range(8):
        at = t * 128
        back = wide[PAD + at + 1 : PAD + at + 129, 0:256] + wide[PAD + at : PAD + at + 128, 256:512]
        back = back + wide[PAD + at - 1 : PAD + at + 127, 512:768]
        grad = back * slope1[at : at + 128, :]
        gb = grad.astype(BF16)
        mixed[0, at : at + 128, :] = gb
        gr = gb.astype(F32)
        turned = [pltpu.roll(gr[:, u * 128 : (u + 1) * 128], 64, 1) for u in range(2)]
        mixed[1, at : at + 128, :] = jnp.concatenate(turned, 1).astype(BF16)
    n, k = iota((256, 256), 0), iota((256, 256), 1)
    odd, r, pair = n // 128, n % 4, (n % 128) // 4
    source = (r // 2) * 128 + ((r + odd) % 2) * 64 + 2 * pair + odd
    order = (k == source).astype(F32).astype(BF16)
    low = lane_is_low(128)
    for t in range(16):
        at = t * 64
        stack = jnp.concatenate(
            [mixed[v, at : at + 64, u * 128 : (u + 1) * 128] for u in range(2) for v in range(2)], 0
        )
        got = dot_n(order, stack)
        out[t * 128 : (t + 1) * 128, :] = jnp.where(low, got[0:128], got[128:256]).astype(BF16)
    prod = dot_0(mixed[0], z[...])
    stem = None
    for r in range(4):
        part = prod[r * 64 : (r + 1) * 64, :]
        places = stem_places(r + 1, 256, True)
        for _ in range(3):
            piece = part.astype(BF16)
            term = dot_t(piece, places)
            stem = term if stem is None else stem + term
            part = part - piece.astype(F32)
    totals[0:448, :] = sums[...]
    totals[256:320, :] = jnp.where(lane_is_low(64), sums[256:320, :], stem[:, 128:256])
    totals[448:512, :] = stem[:, 0:128]


def unpack_kernel(totals, factor, stem_t, conv_t, expand):
    scale = factor[0, 0]
    for u in range(4):
        conv_t[:, u * 128 : (u + 1) * 128] = totals[u * 64 : (u + 1) * 64, :] * scale
    mixed = totals[256:320, :] * scale
    conv_t[:, 512:576] = mixed[:, 0:64]
    stem_t[:, 0:128] = totals[448:512, :] * scale
    stem_t[:, 128:147] = pltpu.roll(mixed, 64, 1)[:, 0:19]
    for u in range(2):
        expand[:, u * 128 : (u + 1) * 128] = totals[320 + u * 64 : 384 + u * 64, :] * scale


def params():
    return pltpu.CompilerParams(vmem_limit_bytes=VMEM_LIMIT)


def shapes(*pairs):
    return [jax.ShapeDtypeStruct(shape, dtype) for shape, dtype in pairs]


SMEM = pl.BlockSpec(memory_space=pltpu.SMEM)
WHOLE = pl.BlockSpec(memory_space=pltpu.VMEM)


def prepare(tissue, cot, stem_t, conv_t, expand):
    def fixed(shape):
        return pl.BlockSpec(shape, lambda i: (0, 0))

    return pl.pallas_call(
        prepare_kernel,
        grid=(4,),
        in_specs=[SMEM, pl.BlockSpec((2048, 128), lambda i: (i, 0)), fixed((64, 256)), fixed((64, 576)), fixed((64, 256))],
        out_specs=[
            pl.BlockSpec((256, 1024), lambda i: (i, 0)),
            pl.BlockSpec((256, 256), lambda i: (i, 0)),
            fixed((384, 512)),
            fixed((256, 1152)),
            fixed((384, 768)),
        ],
        out_shape=shapes(((1024, 1024), BF16), ((1024, 256), F32), ((384, 512), BF16), ((256, 1152), BF16), ((384, 768), BF16)),
        scratch_shapes=[pltpu.VMEM((256, 256), BF16), pltpu.VMEM((256, 1024), BF16)],
        compiler_params=params(),
        name="prepare",
    )(tissue, cot, stem_t, conv_t, expand)


def forward(tissue, place, before, own, after, w1, w2, back2):
    return pl.pallas_call(
        forward_kernel,
        in_specs=[SMEM, SMEM] + [WHOLE] * 6,
        out_specs=[WHOLE] * 6,
        out_shape=shapes(
            ((1024, 512), BF16), ((1024, 1152), BF16), ((1024, 256), F32), ((1024, 256), BF16), ((1024, 256), BF16), ((2, 512, 128), BF16)
        ),
        scratch_shapes=[pltpu.VMEM((64, 2048), F32), pltpu.VMEM((1024 + 2 * PAD, 128), F32), pltpu.VMEM((1024 + 2 * PAD, 384), F32)],
        compiler_params=params(),
        name="forward",
    )(tissue, place, before, own, after, w1, w2, back2)


def filters(act_sh, act2, grad2, cot_f):
    return pl.pallas_call(
        filters_kernel,
        in_specs=[WHOLE] * 4,
        out_specs=WHOLE,
        out_shape=jax.ShapeDtypeStruct((448, 128), F32),
        compiler_params=params(),
        name="filters",
    )(act_sh, act2, grad2, cot_f)


def backward(z, slope1, grad2, halo_a, halo_b, w2b, sums):
    return pl.pallas_call(
        backward_kernel,
        in_specs=[WHOLE] * 7,
        out_specs=[WHOLE] * 2,
        out_shape=shapes(((2048, 128), BF16), ((512, 128), F32)),
        scratch_shapes=[pltpu.VMEM((1024 + 2 * PAD, 768), F32), pltpu.VMEM((2, 1024, 256), BF16)],
        compiler_params=params(),
        name="backward",
    )(z, slope1, grad2, halo_a, halo_b, w2b, sums)


def unpack(totals, factor):
    return pl.pallas_call(
        unpack_kernel,
        in_specs=[WHOLE, SMEM],
        out_specs=[WHOLE] * 3,
        out_shape=shapes(((64, 147), F32), ((64, 576), F32), ((64, 256), F32)),
        compiler_params=params(),
        name="unpack",
    )(totals, factor)


def reduce_all(totals):
    slide = ("x", "y", "core")
    count, depth = lax.axis_size(slide), lax.axis_size("tile")
    part = lax.all_to_all(totals.reshape(count, -1, 128), slide, 0, 0, tiled=True).sum(0)
    part = lax.all_to_all(jnp.broadcast_to(part[None], (depth,) + part.shape), "tile", 0, 0, tiled=True).sum(0)
    whole = lax.all_to_all(jnp.broadcast_to(part[None], (count,) + part.shape), slide, 0, 0, tiled=True)
    return whole.reshape(totals.shape)


def per_device(image, stem_weight, conv_weight, expand_weight, cotangent, tissue):
    depth = lax.axis_size("tile")
    position = lax.axis_index("tile")
    down = [(i, i + 1) for i in range(depth - 1)]
    up = [(i + 1, i) for i in range(depth - 1)]
    before = lax.ppermute(image, "tile", down)
    after = lax.ppermute(image, "tile", up)
    place = jnp.stack([position > 0, position < depth - 1]).astype(jnp.int32)[None]
    rows = tissue[0]
    cot = cotangent[0].reshape(4, 1024, 2, 128).transpose(1, 2, 0, 3).reshape(8192, 128)
    stem_t = jnp.pad(stem_weight.T, ((0, 0), (0, 109)))
    cot_f, back2, w1, w2, w2b = prepare(rows, cot, stem_t, conv_weight.T, expand_weight)
    z, act_sh, slope1, act2, grad2, edge = forward(rows, place, before, image, after, w1, w2, back2)
    halo_b = lax.ppermute(edge[0], "tile", up)
    halo_a = lax.ppermute(edge[1], "tile", down)
    sums = filters(act_sh, act2, grad2, cot_f)
    out, totals = backward(z, slope1, grad2, halo_a, halo_b, w2b, sums)
    totals = reduce_all(totals)
    factor = jnp.full((1, 1), 1.0 / 1024.0, F32)
    stem_g, conv_g, expand_g = unpack(totals, factor)
    field = out.reshape(512, 4, 128).transpose(1, 0, 2)
    field = with_layout_constraint(field, Layout(major_to_minor=(1, 0, 2)))
    return field.reshape(1, 4, 65536), stem_g.T, conv_g.T, expand_g


def solution(mesh):
    slide = ("x", "y", "core")
    fine = Mesh(mesh.devices.reshape(4, 4, 2, 8), slide + ("tile",))
    placed = (P(slide, None, "tile", None), P(), P(), P(), P(slide, "tile", None), P(slide, None, None))
    return jax.shard_map(
        per_device, mesh=fine, in_specs=placed, out_specs=(P(slide, "tile", None), P(), P(), P()), check_vma=False
    )
```

```python
import jax
import jax.numpy as jnp
from jax import lax
from jax.experimental import pallas as pl
from jax.experimental.layout import Layout, with_layout_constraint
from jax.experimental.pallas import tpu as pltpu
from jax.sharding import Mesh, PartitionSpec as P

F32 = jnp.float32
BF16 = jnp.bfloat16
VMEM_LIMIT = 56 * 1024 * 1024

ROWS = (0, 1, 2, 3, -1, 4, -2, 5)
PAD = 8
CHUNKS = 8
WIDE = 128


def dot_0(left, right):
    return lax.dot_general(left, right, (((0,), (0,)), ((), ())), preferred_element_type=F32)


def dot_t(left, right):
    return lax.dot_general(left, right, (((1,), (1,)), ((), ())), preferred_element_type=F32)


def dot_n(left, right):
    return jnp.dot(left, right, preferred_element_type=F32)


def iota(shape, dim):
    return lax.broadcasted_iota(jnp.int32, shape, dim)


def lane_is_low(rows):
    return iota((rows, 128), 1) < 64


def turn(value):
    return pltpu.roll(value, 64, 1)


def sigmoid(value):
    return 1.0 / (1.0 + jnp.exp(-value))


def stem_places(row, split):
    place = iota((512, 1), 0)
    tap = place // 64
    within = place % 64
    colour = (within >= 21).astype(jnp.int32) + (within >= 42).astype(jnp.int32)
    line = within - 21 * colour - (2 * row + 4)
    valid = (tap >= 1) & (within < 63) & (line >= 0) & (line <= 6)
    entry = line * 21 + (tap - 1) * 3 + colour
    if split:
        entry = jnp.where(entry < 128, entry, entry + 64)
    entry = jnp.where(valid, entry, -1)
    return (iota((512, 256), 1) == entry).astype(F32).astype(BF16)


def edges_kernel(tissue, cot, image, expand, up, down, order, wide, rows):
    step = pl.program_id(0)

    @pl.when(step == 0)
    def _():
        m, k = iota((128, 256), 0), iota((128, 256), 1)
        source = (m % 32) * 8 + ((m // 32) % 2) * 4 + (m // 64) * 3
        order[...] = (k == source).astype(F32).astype(BF16)
        both = jnp.concatenate([expand[...].astype(F32)] * 2, 0).T
        low = lane_is_low(256)
        wide[0:256, :] = jnp.where(low, both, 0.0).astype(BF16)
        wide[256:512, :] = jnp.where(low, 0.0, both).astype(BF16)

    for s in range(8):
        got = dot_n(order[...], cot[s * 256 : (s + 1) * 256, :]).astype(BF16)
        for n in range(4):
            rows[s * 32 : (s + 1) * 32, n * 128 : (n + 1) * 128] = got[n * 32 : (n + 1) * 32, :]
    back = dot_n(rows[...], wide[...]) * tissue[0, step].astype(F32)
    low = lane_is_low(128)
    a, b = back[0:128], back[128:256]
    first = jnp.where(low, a, turn(b)).astype(BF16)
    last = jnp.where(low, turn(a), b).astype(BF16)
    for v in range(4):
        up[0:32, v * 128 : (v + 1) * 128] = first[v * 32 : (v + 1) * 32, :]
        down[0:32, v * 128 : (v + 1) * 128] = last[v * 32 : (v + 1) * 32, :]
    for k in range(3):
        up[32 + 8 * k : 40 + 8 * k, :] = image[0, k]
        down[32 + 8 * k : 40 + 8 * k, :] = image[0, k]


def prepare_kernel(tissue, cot, expand, stem_t, conv_t, cot_f, back2, w1, w2, w2b, order, wide, filt):
    step = pl.program_id(0)

    @pl.when(step == 0)
    def _():
        m, k = iota((256, 256), 0), iota((256, 256), 1)
        source = (m % 32) * 8 + ((m // 32) % 2) * 4 + m // 64
        order[...] = (k == source).astype(F32).astype(BF16)
        wide[...] = jnp.zeros(wide.shape, BF16)
        both = jnp.concatenate([expand[...].astype(F32)] * 2, 0).T
        low = lane_is_low(256)
        for r in range(4):
            keep = low if r % 2 == 0 else jnp.logical_not(low)
            wide[r * 256 : (r + 1) * 256, (r // 2) * 128 : (r // 2 + 1) * 128] = jnp.where(keep, both, 0.0).astype(BF16)

    @pl.when(step == 1)
    def _():
        filt[...] = jnp.zeros(filt.shape, F32)
        filt[0:64, 0:147] = stem_t[...].astype(F32)
        both = filt[0:64, 0:256]
        both = jnp.concatenate([both, both], 0).T
        low = lane_is_low(256)
        halves = [jnp.where(low, both, 0.0).astype(BF16), jnp.where(low, 0.0, both).astype(BF16)]
        for t in range(4):
            tile = dot_n(stem_places(ROWS[2 * t], False), halves[0]) + dot_n(stem_places(ROWS[2 * t + 1], False), halves[1])
            w1[:, t * 128 : (t + 1) * 128] = tile.astype(BF16)

    @pl.when(step == 2)
    def _():
        filt[0:64, 0:576] = conv_t[...].astype(F32)
        filt[64:128, 0:576] = conv_t[...].astype(F32)
        turned = filt[...].T
        low = lane_is_low(64)
        flat = jnp.zeros((64, 128), F32)

        def pair(i0, i1, j):
            tiles = [turned[(3 * i + j) * 64 : (3 * i + j + 1) * 64, :] if 0 <= i <= 2 else flat for i in (i0, i1)]
            return jnp.where(low, tiles[0], tiles[1]).astype(BF16)

        for j in range(3):
            for a in range(8):
                base = j * 384 + a * 64 if a < 6 else 1152 + j * 128 + (a - 6) * 64
                for t in range(3):
                    i0, i1 = (ROWS[a] - ROWS[2 * t + e] + 1 for e in range(2))
                    w2[base : base + 64, t * 128 : (t + 1) * 128] = pair(i0, i1, j)

    @pl.when(step == 3)
    def _():
        blocks = [conv_t[:, n * 64 : (n + 1) * 64].astype(F32) for n in range(9)]
        empty = jnp.zeros((64, 64), F32)

        def block(i, j):
            return blocks[3 * i + j] if 0 <= i <= 2 else empty

        for j in range(3):
            for slot in range(6):
                for t in range(2):
                    tile = jnp.concatenate([block(2 * t + e - ROWS[slot] + 1, j) for e in range(2)], 1)
                    w2b[slot * 64 : (slot + 1) * 64, j * 256 + t * 128 : j * 256 + (t + 1) * 128] = tile.astype(BF16)

    for s in range(8):
        got = dot_n(order[...], cot[s * 256 : (s + 1) * 256, :]).astype(BF16)
        for n in range(8):
            cot_f[s * 32 : (s + 1) * 32, n * 128 : (n + 1) * 128] = got[n * 32 : (n + 1) * 32, :]
    back2[...] = dot_n(cot_f[...], wide[...]) * tissue[0, step].astype(F32)


def main_kernel(
    tissue, place, own_i, before_i, after_i, w1_i, w2_i, back2_i, w2b_i, cot_i, out_o, totals,
    own, before, after, w1, w2, back2, w2b, cot_f,
    lines, cols, z, act, slope1, act_sh, act2, grad2, wide, mixed, out, sems,
):
    count = [0]

    def fetch(src, dst):
        copy = pltpu.make_async_copy(src, dst, sems.at[count[0]])
        copy.start()
        count[0] += 1
        return copy

    in_image = [fetch(own_i, own), fetch(before_i, before), fetch(after_i, after)]
    in_w1 = fetch(w1_i, w1)
    in_w2 = fetch(w2_i, w2)
    in_back = [fetch(back2_i, back2), fetch(w2b_i, w2b)]
    in_cot = fetch(cot_i, cot_f)

    m, x = iota((128, 512), 0), iota((128, 512), 1)
    pick = (x == jnp.where(x < 256, 2 * m, 2 * m + 257)).astype(F32).astype(BF16)
    cols[0:PAD, :] = jnp.zeros((PAD, 128), F32)
    cols[PAD + 1024 :, :] = jnp.zeros((PAD, 128), F32)
    act[0:PAD, :] = jnp.zeros((PAD, 512), F32)
    act[PAD + 1024 :, :] = jnp.zeros((PAD, 512), F32)
    wide[0:PAD, :] = jnp.zeros((PAD, 768), F32)
    wide[PAD + 1024 :, :] = jnp.zeros((PAD, 768), F32)
    lines[63:64, :] = jnp.zeros((1, 2048), F32)
    none = jnp.zeros((64, 256), BF16)
    for copy in in_image:
        copy.wait()
    for k in range(3):
        lines[21 * k : 21 * k + 7, :] = before[32 + 8 * k : 40 + 8 * k, :].astype(F32)[1:8]
        lines[21 * k + 7 : 21 * k + 15, :] = own[0, k].astype(F32)
        lines[21 * k + 15 : 21 * k + 21, :] = after[32 + 8 * k : 40 + 8 * k, :].astype(F32)[0:6]
    for t in range(8):
        part = lines[:, t * 256 : (t + 1) * 256].astype(BF16)
        spread = jnp.concatenate([jnp.concatenate([part, none], 0), jnp.concatenate([none, part], 0)], 1)
        cols[PAD + t * 128 : PAD + (t + 1) * 128, :] = dot_t(pick, spread)

    ends = jnp.where(lane_is_low(1), place[0, 0].astype(F32), place[0, 1].astype(F32))
    in_w1.wait()
    for t in range(CHUNKS):
        at = t * WIDE
        wins = [cols[PAD + at + s : PAD + at + s + WIDE, :].astype(BF16) for s in (-2, -1, 0, 1)]
        zt = jnp.concatenate(wins, 1)
        z[at : at + WIDE, :] = zt
        pre = dot_n(zt, w1[...])
        sig = sigmoid(pre)
        value = pre * sig
        act[PAD + at : PAD + at + WIDE, 0:256] = value[:, :256]
        act[PAD + at : PAD + at + WIDE, 256:384] = value[:, 256:384] * ends
        act[PAD + at : PAD + at + WIDE, 384:512] = value[:, 384:512] * ends
        slope1[at : at + WIDE, :] = (sig * (1.0 + pre * (1.0 - sig)))[:, :256]

    low = lane_is_low(WIDE)
    in_w2.wait()
    for copy in in_back:
        copy.wait()
    for t in range(CHUNKS):
        at = t * WIDE
        wins = [act[PAD + at + j - 1 : PAD + at + j - 1 + WIDE, :].astype(BF16) for j in range(3)]
        near = jnp.concatenate([win[:, :384] for win in wins], 1)
        act_sh[at : at + WIDE, :] = near
        pre = dot_n(jnp.concatenate([near] + [win[:, 384:] for win in wins], 1), w2[...])
        sig = sigmoid(pre)
        keep = tissue[0, t // 2].astype(F32)
        act2[at : at + WIDE, :] = (pre * sig * keep)[:, :256].astype(BF16)
        slope = sig * (1.0 + pre * (1.0 - sig))
        grad2[at : at + WIDE, 0:256] = (back2[at : at + WIDE, :] * slope[:, :256]).astype(BF16)
        tiles = [(t // 2) * 4 + v for v in range(4)]
        a, b = (jnp.concatenate([ref[0:32, v * 128 : (v + 1) * 128] for v in tiles], 0).astype(F32) for ref in (before, after))
        ends = jnp.where(low, turn(a), b) if t % 2 else jnp.where(low, a, turn(b))
        grad2[at : at + WIDE, 256:384] = (ends * slope[:, 256:384]).astype(BF16)
        wide[PAD + at : PAD + at + WIDE, :] = dot_n(grad2[at : at + WIDE, :], w2b[...])

    for t in range(CHUNKS):
        at = t * WIDE
        back = wide[PAD + at + 1 : PAD + at + 1 + WIDE, 0:256] + wide[PAD + at : PAD + at + WIDE, 256:512]
        back = back + wide[PAD + at - 1 : PAD + at - 1 + WIDE, 512:768]
        gb = (back * slope1[at : at + WIDE, :]).astype(BF16)
        mixed[0, at : at + WIDE, :] = gb
        gr = gb.astype(F32)
        mixed[1, at : at + WIDE, :] = jnp.concatenate([turn(gr[:, :128]), turn(gr[:, 128:])], 1).astype(BF16)

    n, k = iota((256, 256), 0), iota((256, 256), 1)
    odd, r, two = n // 128, n % 4, (n % 128) // 4
    source = (r // 2) * 128 + ((r + odd) % 2) * 64 + 2 * two + odd
    order = (k == source).astype(F32).astype(BF16)
    for t in range(16):
        at = t * 64
        stack = jnp.concatenate([mixed[v, at : at + 64, u * 128 : (u + 1) * 128] for u in range(2) for v in range(2)], 0)
        got = dot_n(order, stack)
        out[t * 128 : (t + 1) * 128, :] = jnp.where(low, got[0:128], got[128:256]).astype(BF16)
    out_copy = fetch(out, out_o)

    scale = 1.0 / 1024.0
    low = lane_is_low(64)
    prod = dot_0(grad2[:, 0:256], act_sh[...]) * scale
    halves = {}
    for i in range(3):
        for j in range(3):
            at_low, at_high = [], []
            for r in range(4):
                slot = ROWS.index(r + i - 1)
                col = j * 384 + (slot // 2) * 128
                tile = prod[r * 64 : (r + 1) * 64, col : col + 128]
                (at_high if slot % 2 else at_low).append(tile)
            halves[3 * i + j] = (sum(at_low[1:], at_low[0]), sum(at_high[1:], at_high[0]))
    last = None
    for u in range(5):
        a, b = halves[2 * u]
        left = a + turn(b)
        if u == 4:
            last = left
        else:
            a, b = halves[2 * u + 1]
            totals[u * 64 : (u + 1) * 64, :] = jnp.where(low, left, turn(a) + b)

    in_cot.wait()
    total = None
    for t in range(2):
        both = dot_0(act2[:, t * 128 : (t + 1) * 128], cot_f[:, t * 512 : (t + 1) * 512])
        part = both[0:64, 0:256] + both[64:128, 256:512]
        total = part if total is None else total + part
    total = total * scale
    totals[320:384, :] = total[:, 0:128]
    totals[384:448, :] = total[:, 128:256]

    prod = dot_0(mixed[0], z[...]) * scale
    stem = None
    for r in range(4):
        part = prod[r * 64 : (r + 1) * 64, :]
        pieces = []
        for _ in range(3):
            piece = part.astype(BF16)
            pieces.append(piece)
            part = part - piece.astype(F32)
        term = dot_n(jnp.concatenate(pieces, 0), stem_places(r, True))
        term = term[0:64] + term[64:128] + term[128:192]
        stem = term if stem is None else stem + term
    totals[256:320, :] = jnp.where(low, last, stem[:, 128:256])
    totals[448:512, :] = stem[:, 0:128]
    out_copy.wait()


def unpack_kernel(totals, stem_t, conv_t, expand):
    for u in range(4):
        conv_t[:, u * 128 : (u + 1) * 128] = totals[u * 64 : (u + 1) * 64, :]
    mixed = totals[256:320, :]
    conv_t[:, 512:576] = mixed[:, 0:64]
    stem_t[:, 0:128] = totals[448:512, :]
    stem_t[:, 128:147] = turn(mixed)[:, 0:19]
    for u in range(2):
        expand[:, u * 128 : (u + 1) * 128] = totals[320 + u * 64 : 384 + u * 64, :]


def params():
    return pltpu.CompilerParams(vmem_limit_bytes=VMEM_LIMIT)


def shapes(*pairs):
    return [jax.ShapeDtypeStruct(shape, dtype) for shape, dtype in pairs]


SMEM = pl.BlockSpec(memory_space=pltpu.SMEM)
WHOLE = pl.BlockSpec(memory_space=pltpu.VMEM)
APART = pl.BlockSpec(memory_space=pl.ANY)


def prepare(tissue, cot, expand, stem_t, conv_t):
    def part(rows, lanes):
        return pl.BlockSpec((rows, lanes), lambda i: (i, 0))

    def fixed(rows, lanes):
        return pl.BlockSpec((rows, lanes), lambda i: (0, 0))

    return pl.pallas_call(
        prepare_kernel,
        grid=(4,),
        in_specs=[SMEM, part(2048, 128), fixed(64, 256), fixed(64, 147), fixed(64, 576)],
        out_specs=[part(256, 1024), part(256, 256), fixed(512, 512), fixed(1536, 384), fixed(384, 768)],
        out_shape=shapes(((1024, 1024), BF16), ((1024, 256), F32), ((512, 512), BF16), ((1536, 384), BF16), ((384, 768), BF16)),
        scratch_shapes=[pltpu.VMEM((256, 256), BF16), pltpu.VMEM((1024, 256), BF16), pltpu.VMEM((128, 640), F32)],
        compiler_params=params(),
        name="prepare",
    )(tissue, cot, expand, stem_t, conv_t)


def edges(tissue, cot, image, expand):
    return pl.pallas_call(
        edges_kernel,
        grid=(4,),
        in_specs=[
            SMEM,
            pl.BlockSpec((2048, 128), lambda i: (i, 0)),
            pl.BlockSpec((1, 3, 8, 512), lambda i: (0, 0, 0, i)),
            pl.BlockSpec((64, 256), lambda i: (0, 0)),
        ],
        out_specs=[pl.BlockSpec((56, 512), lambda i: (0, i))] * 2,
        out_shape=shapes(((56, 2048), BF16), ((56, 2048), BF16)),
        scratch_shapes=[pltpu.VMEM((128, 256), BF16), pltpu.VMEM((512, 128), BF16), pltpu.VMEM((256, 512), BF16)],
        compiler_params=params(),
        name="edges",
    )(tissue, cot, image, expand)


def main(tissue, place, own, before, after, w1, w2, back2, w2b, cot_f):
    return pl.pallas_call(
        main_kernel,
        in_specs=[SMEM, SMEM] + [APART] * 8,
        out_specs=[APART, WHOLE],
        out_shape=shapes(((2048, 128), BF16), ((512, 128), F32)),
        scratch_shapes=[
            pltpu.VMEM((1, 3, 8, 2048), BF16),
            pltpu.VMEM((56, 2048), BF16),
            pltpu.VMEM((56, 2048), BF16),
            pltpu.VMEM((512, 512), BF16),
            pltpu.VMEM((1536, 384), BF16),
            pltpu.VMEM((1024, 256), F32),
            pltpu.VMEM((384, 768), BF16),
            pltpu.VMEM((1024, 1024), BF16),
            pltpu.VMEM((64, 2048), F32),
            pltpu.VMEM((1024 + 2 * PAD, 128), F32),
            pltpu.VMEM((1024, 512), BF16),
            pltpu.VMEM((1024 + 2 * PAD, 512), F32),
            pltpu.VMEM((1024, 256), F32),
            pltpu.VMEM((1024, 1152), BF16),
            pltpu.VMEM((1024, 256), BF16),
            pltpu.VMEM((1024, 384), BF16),
            pltpu.VMEM((1024 + 2 * PAD, 768), F32),
            pltpu.VMEM((2, 1024, 256), BF16),
            pltpu.VMEM((2048, 128), BF16),
            pltpu.SemaphoreType.DMA((10,)),
        ],
        compiler_params=params(),
        name="main",
    )(tissue, place, own, before, after, w1, w2, back2, w2b, cot_f)


def unpack(totals):
    return pl.pallas_call(
        unpack_kernel,
        in_specs=[WHOLE],
        out_specs=[WHOLE] * 3,
        out_shape=shapes(((64, 147), F32), ((64, 576), F32), ((64, 256), F32)),
        compiler_params=params(),
        name="unpack",
    )(totals)


def reduce_all(totals):
    slide = ("x", "y", "core")
    count, depth = lax.axis_size(slide), lax.axis_size("tile")
    part = lax.all_to_all(totals.reshape(count, -1, 128), slide, 0, 0, tiled=True).sum(0)
    part = lax.all_to_all(jnp.broadcast_to(part[None], (depth,) + part.shape), "tile", 0, 0, tiled=True).sum(0)
    whole = lax.all_to_all(jnp.broadcast_to(part[None], (count,) + part.shape), slide, 0, 0, tiled=True)
    return whole.reshape(totals.shape)


def per_device(image, stem_weight, conv_weight, expand_weight, cotangent, tissue):
    depth = lax.axis_size("tile")
    position = lax.axis_index("tile")
    rows = tissue[0]
    cot = cotangent[0].reshape(4, 1024, 2, 128).transpose(1, 2, 0, 3).reshape(8192, 128)
    up, down = edges(rows, cot, image, expand_weight)
    before = lax.ppermute(down, "tile", [(i, i + 1) for i in range(depth - 1)])
    after = lax.ppermute(up, "tile", [(i + 1, i) for i in range(depth - 1)])
    place = jnp.stack([position > 0, position < depth - 1]).astype(jnp.int32)[None]
    cot_f, back2, w1, w2, w2b = prepare(rows, cot, expand_weight, stem_weight.T, conv_weight.T)
    out, totals = main(rows, place, image, before, after, w1, w2, back2, w2b, cot_f)
    stem_g, conv_g, expand_g = unpack(reduce_all(totals))
    field = out.reshape(512, 4, 128).transpose(1, 0, 2)
    field = with_layout_constraint(field, Layout(major_to_minor=(1, 0, 2)))
    return field.reshape(1, 4, 65536), stem_g.T, conv_g.T, expand_g


def solution(mesh):
    slide = ("x", "y", "core")
    fine = Mesh(mesh.devices.reshape(4, 4, 2, 8), slide + ("tile",))
    placed = (P(slide, None, "tile", None), P(), P(), P(), P(slide, "tile", None), P(slide, None, None))
    return jax.shard_map(
        per_device, mesh=fine, in_specs=placed, out_specs=(P(slide, "tile", None), P(), P(), P()), check_vma=False
    )
```

```python
import jax
import jax.numpy as jnp
from jax import lax
from jax.experimental import pallas as pl
from jax.experimental.layout import Layout, with_layout_constraint
from jax.experimental.pallas import tpu as pltpu
from jax.sharding import Mesh, PartitionSpec as P

F32 = jnp.float32
BF16 = jnp.bfloat16
VMEM_LIMIT = 56 * 1024 * 1024

ROWS = (0, 1, 2, 3, -1, 4, -2, 5)
PAD = 8
CHUNKS = 8
WIDE = 128
SPAN = 256


def dot_0(left, right):
    return lax.dot_general(left, right, (((0,), (0,)), ((), ())), preferred_element_type=F32)


def dot_t(left, right):
    return lax.dot_general(left, right, (((1,), (1,)), ((), ())), preferred_element_type=F32)


def dot_n(left, right):
    return jnp.dot(left, right, preferred_element_type=F32)


def iota(shape, dim):
    return lax.broadcasted_iota(jnp.int32, shape, dim)


def lane_is_low(rows):
    return iota((rows, 128), 1) < 64


def turn(value):
    return pltpu.roll(value, 64, 1)


def sigmoid(value):
    return 1.0 / (1.0 + jnp.exp(-value))


def stem_places(row, split):
    place = iota((512, 1), 0)
    tap = place // 64
    within = place % 64
    colour = (within >= 21).astype(jnp.int32) + (within >= 42).astype(jnp.int32)
    line = within - 21 * colour - (2 * row + 4)
    valid = (tap >= 1) & (within < 63) & (line >= 0) & (line <= 6)
    entry = line * 21 + (tap - 1) * 3 + colour
    if split:
        entry = jnp.where(entry < 128, entry, entry + 64)
    entry = jnp.where(valid, entry, -1)
    return (iota((512, 256), 1) == entry).astype(F32).astype(BF16)


def is_even():
    return lax.axis_index("tile") % 2 == 0


def fetcher(sems):
    count = [0]

    def fetch(src, dst):
        copy = pltpu.make_async_copy(src, dst, sems.at[count[0]])
        copy.start()
        count[0] += 1
        return copy

    return fetch


def edges_kernel(tissue, cot_i, image, expand, to_first, to_second, cot, rows, sems):
    even = is_even()
    fetch = fetcher(sems)
    parts = [fetch(cot_i.at[pl.ds(q * 2048, 2048)], cot.at[pl.ds(q * 2048, 2048)]) for q in range(4)]
    for k in range(3):
        to_first[32 + 8 * k : 40 + 8 * k, :] = image[0, k]
        to_second[32 + 8 * k : 40 + 8 * k, :] = image[0, k]
    m, k = iota((128, 256), 0), iota((128, 256), 1)
    source = (m % 32) * 8 + ((m // 32) % 2) * 4 + (m // 64) * 3
    order = (k == source).astype(F32).astype(BF16)
    both = jnp.concatenate([expand[...].astype(F32)] * 2, 0).T
    low = lane_is_low(256)
    wide = jnp.concatenate([jnp.where(low, both, 0.0), jnp.where(low, 0.0, both)], 0).astype(BF16)
    low = lane_is_low(128)
    for q in range(4):
        parts[q].wait()
        for s in range(8):
            got = dot_n(order, cot[q * 2048 + s * 256 : q * 2048 + (s + 1) * 256, :]).astype(BF16)
            for n in range(4):
                rows[q * 256 + s * 32 : q * 256 + (s + 1) * 32, n * 128 : (n + 1) * 128] = got[n * 32 : (n + 1) * 32, :]
        back = dot_n(rows[q * 256 : (q + 1) * 256, :], wide) * tissue[0, q].astype(F32)
        a, b = back[0:128], back[128:256]
        top = jnp.where(low, a, turn(b))
        bottom = jnp.where(low, turn(a), b)
        first = jnp.where(even, bottom, top).astype(BF16)
        second = jnp.where(even, top, bottom).astype(BF16)
        for v in range(4):
            u = q * 4 + v
            to_first[0:32, u * 128 : (u + 1) * 128] = first[v * 32 : (v + 1) * 32, :]
            to_second[0:32, u * 128 : (u + 1) * 128] = second[v * 32 : (v + 1) * 32, :]


def prepare_kernel(
    tissue, cot_i, expand, stem_t, conv_t, cot_o, back2_o, w1_o, w2_o, w2b_o,
    cot, cot_f, back2, w1, w2, w2b, wide, filt, sems,
):
    fetch = fetcher(sems)
    parts = [fetch(cot_i.at[pl.ds(q * 2048, 2048)], cot.at[pl.ds(q * 2048, 2048)]) for q in range(4)]
    sent = []

    filt[...] = jnp.zeros(filt.shape, F32)
    filt[0:64, 0:147] = stem_t[...].astype(F32)
    both = filt[0:64, 0:256]
    both = jnp.concatenate([both, both], 0).T
    low = lane_is_low(256)
    halves = [jnp.where(low, both, 0.0).astype(BF16), jnp.where(low, 0.0, both).astype(BF16)]
    for t in range(4):
        tile = dot_n(stem_places(ROWS[2 * t], False), halves[0]) + dot_n(stem_places(ROWS[2 * t + 1], False), halves[1])
        w1[:, t * 128 : (t + 1) * 128] = tile.astype(BF16)
    sent.append(fetch(w1, w1_o))

    filt[0:64, 0:576] = conv_t[...].astype(F32)
    filt[64:128, 0:576] = conv_t[...].astype(F32)
    turned = filt[...].T
    low = lane_is_low(64)
    flat = jnp.zeros((64, 128), F32)

    def pair(i0, i1, j):
        tiles = [turned[(3 * i + j) * 64 : (3 * i + j + 1) * 64, :] if 0 <= i <= 2 else flat for i in (i0, i1)]
        return jnp.where(low, tiles[0], tiles[1]).astype(BF16)

    for j in range(3):
        for a in range(8):
            base = j * 384 + a * 64 if a < 6 else 1152 + j * 128 + (a - 6) * 64
            for t in range(3):
                i0, i1 = (ROWS[a] - ROWS[2 * t + e] + 1 for e in range(2))
                w2[base : base + 64, t * 128 : (t + 1) * 128] = pair(i0, i1, j)
    sent.append(fetch(w2, w2_o))
    blocks = [conv_t[:, n * 64 : (n + 1) * 64].astype(F32) for n in range(9)]
    empty = jnp.zeros((64, 64), F32)

    def block(i, j):
        return blocks[3 * i + j] if 0 <= i <= 2 else empty

    for j in range(3):
        for slot in range(6):
            for t in range(2):
                tile = jnp.concatenate([block(2 * t + e - ROWS[slot] + 1, j) for e in range(2)], 1)
                w2b[slot * 64 : (slot + 1) * 64, j * 256 + t * 128 : j * 256 + (t + 1) * 128] = tile.astype(BF16)
    sent.append(fetch(w2b, w2b_o))

    m, k = iota((256, 256), 0), iota((256, 256), 1)
    source = (m % 32) * 8 + ((m // 32) % 2) * 4 + m // 64
    order = (k == source).astype(F32).astype(BF16)
    wide[...] = jnp.zeros(wide.shape, BF16)
    both = jnp.concatenate([expand[...].astype(F32)] * 2, 0).T
    low = lane_is_low(256)
    for r in range(4):
        keep = low if r % 2 == 0 else jnp.logical_not(low)
        wide[r * 256 : (r + 1) * 256, (r // 2) * 128 : (r // 2 + 1) * 128] = jnp.where(keep, both, 0.0).astype(BF16)
    for q in range(4):
        parts[q].wait()
        for s in range(8):
            got = dot_n(order, cot[q * 2048 + s * 256 : q * 2048 + (s + 1) * 256, :]).astype(BF16)
            for n in range(8):
                cot_f[q * 256 + s * 32 : q * 256 + (s + 1) * 32, n * 128 : (n + 1) * 128] = got[n * 32 : (n + 1) * 32, :]
        part = pl.ds(q * 256, 256)
        back2[part, :] = dot_n(cot_f[part, :], wide[...]) * tissue[0, q].astype(F32)
        sent.append(fetch(cot_f.at[part], cot_o.at[part]))
        sent.append(fetch(back2.at[part], back2_o.at[part]))
    for copy in sent:
        copy.wait()


def main_kernel(
    tissue, own_i, first_i, second_i, w1_i, w2_i, back2_i, w2b_i, cot_i, out_o, totals,
    own, before, after, w1, w2, back2, w2b, cot_f,
    lines, cols, z, act, slope1, act_sh, act2, grad2, wide, mixed, out, sems,
):
    fetch = fetcher(sems)
    even = is_even()

    @pl.when(even)
    def _():
        pltpu.make_async_copy(second_i, before, sems.at[8]).start()
        pltpu.make_async_copy(first_i, after, sems.at[9]).start()

    @pl.when(jnp.logical_not(even))
    def _():
        pltpu.make_async_copy(first_i, before, sems.at[8]).start()
        pltpu.make_async_copy(second_i, after, sems.at[9]).start()

    in_image = [fetch(own_i, own)]
    in_image += [pltpu.make_async_copy(first_i, before, sems.at[8]), pltpu.make_async_copy(second_i, after, sems.at[9])]
    in_w1 = fetch(w1_i, w1)
    in_w2 = fetch(w2_i, w2)
    in_back = [fetch(back2_i, back2), fetch(w2b_i, w2b)]
    in_cot = fetch(cot_i, cot_f)

    m, x = iota((128, 512), 0), iota((128, 512), 1)
    pick = (x == jnp.where(x < 256, 2 * m, 2 * m + 257)).astype(F32).astype(BF16)
    cols[0:PAD, :] = jnp.zeros((PAD, 128), F32)
    cols[PAD + 1024 :, :] = jnp.zeros((PAD, 128), F32)
    act[0:PAD, :] = jnp.zeros((PAD, 512), F32)
    act[PAD + 1024 :, :] = jnp.zeros((PAD, 512), F32)
    wide[0:PAD, :] = jnp.zeros((PAD, 768), F32)
    wide[PAD + 1024 :, :] = jnp.zeros((PAD, 768), F32)
    lines[63:64, :] = jnp.zeros((1, 2048), F32)
    none = jnp.zeros((64, 256), BF16)
    for copy in in_image:
        copy.wait()
    for k in range(3):
        lines[21 * k : 21 * k + 7, :] = before[32 + 8 * k : 40 + 8 * k, :].astype(F32)[1:8]
        lines[21 * k + 7 : 21 * k + 15, :] = own[0, k].astype(F32)
        lines[21 * k + 15 : 21 * k + 21, :] = after[32 + 8 * k : 40 + 8 * k, :].astype(F32)[0:6]
    for t in range(8):
        part = lines[:, t * 256 : (t + 1) * 256].astype(BF16)
        spread = jnp.concatenate([jnp.concatenate([part, none], 0), jnp.concatenate([none, part], 0)], 1)
        cols[PAD + t * 128 : PAD + (t + 1) * 128, :] = dot_t(pick, spread)

    position = lax.axis_index("tile")
    ends = jnp.where(lane_is_low(1), (position > 0).astype(F32), (position < lax.axis_size("tile") - 1).astype(F32))
    in_w1.wait()
    for t in range(CHUNKS):
        at = t * WIDE
        wins = [cols[PAD + at + s : PAD + at + s + WIDE, :].astype(BF16) for s in (-2, -1, 0, 1)]
        zt = jnp.concatenate(wins, 1)
        z[at : at + WIDE, :] = zt
        pre = dot_n(zt, w1[...])
        sig = sigmoid(pre)
        value = pre * sig
        act[PAD + at : PAD + at + WIDE, 0:256] = value[:, :256]
        act[PAD + at : PAD + at + WIDE, 256:384] = value[:, 256:384] * ends
        act[PAD + at : PAD + at + WIDE, 384:512] = value[:, 384:512] * ends
        slope1[at : at + WIDE, :] = (sig * (1.0 + pre * (1.0 - sig)))[:, :256]

    low = lane_is_low(128)
    in_w2.wait()
    for copy in in_back:
        copy.wait()
    for t in range(1024 // SPAN):
        at = t * SPAN
        wins = [act[PAD + at + j - 1 : PAD + at + j - 1 + SPAN, :].astype(BF16) for j in range(3)]
        near = jnp.concatenate([win[:, :384] for win in wins], 1)
        act_sh[at : at + SPAN, :] = near
        pre = dot_n(near, w2[0:1152, 0:256])
        sig = sigmoid(pre)
        keep = tissue[0, at // 256].astype(F32)
        act2[at : at + SPAN, :] = (pre * sig * keep).astype(BF16)
        grad2[at : at + SPAN, 0:256] = (back2[at : at + SPAN, :] * (sig * (1.0 + pre * (1.0 - sig)))).astype(BF16)
        pre = dot_n(jnp.concatenate([near] + [win[:, 384:] for win in wins], 1), w2[:, 256:384])
        sig = sigmoid(pre)
        ends = []
        for u in range(at // 128, (at + SPAN) // 128):
            tiles = [(u // 2) * 4 + v for v in range(4)]
            a, b = (jnp.concatenate([ref[0:32, v * 128 : (v + 1) * 128] for v in tiles], 0).astype(F32) for ref in (before, after))
            ends.append(jnp.where(low, turn(a), b) if u % 2 else jnp.where(low, a, turn(b)))
        slope = sig * (1.0 + pre * (1.0 - sig))
        grad2[at : at + SPAN, 256:384] = (jnp.concatenate(ends, 0) * slope).astype(BF16)
        wide[PAD + at : PAD + at + SPAN, :] = dot_n(grad2[at : at + SPAN, :], w2b[...])

    for t in range(CHUNKS):
        at = t * WIDE
        back = wide[PAD + at + 1 : PAD + at + 1 + WIDE, 0:256] + wide[PAD + at : PAD + at + WIDE, 256:512]
        back = back + wide[PAD + at - 1 : PAD + at - 1 + WIDE, 512:768]
        gb = (back * slope1[at : at + WIDE, :]).astype(BF16)
        mixed[0, at : at + WIDE, :] = gb
        gr = gb.astype(F32)
        mixed[1, at : at + WIDE, :] = jnp.concatenate([turn(gr[:, :128]), turn(gr[:, 128:])], 1).astype(BF16)

    n, k = iota((256, 256), 0), iota((256, 256), 1)
    odd, r, two = n // 128, n % 4, (n % 128) // 4
    source = (r // 2) * 128 + ((r + odd) % 2) * 64 + 2 * two + odd
    order = (k == source).astype(F32).astype(BF16)
    for t in range(8):
        stacks = []
        for at in (t * 128, t * 128 + 64):
            stacks.append(jnp.concatenate([mixed[v, at : at + 64, u * 128 : (u + 1) * 128] for u in range(2) for v in range(2)], 0))
        got = dot_n(order, jnp.concatenate(stacks, 1))
        for e in range(2):
            at = t * 256 + e * 128
            out[at : at + 128, :] = jnp.where(low, got[0:128, e * 128 : e * 128 + 128], got[128:256, e * 128 : e * 128 + 128]).astype(BF16)
    out_copy = fetch(out, out_o)

    scale = 1.0 / 1024.0
    low = lane_is_low(64)
    prod = dot_0(grad2[:, 0:256], act_sh[...]) * scale
    halves = {}
    for i in range(3):
        for j in range(3):
            at_low, at_high = [], []
            for r in range(4):
                slot = ROWS.index(r + i - 1)
                col = j * 384 + (slot // 2) * 128
                tile = prod[r * 64 : (r + 1) * 64, col : col + 128]
                (at_high if slot % 2 else at_low).append(tile)
            halves[3 * i + j] = (sum(at_low[1:], at_low[0]), sum(at_high[1:], at_high[0]))
    last = None
    for u in range(5):
        a, b = halves[2 * u]
        left = a + turn(b)
        if u == 4:
            last = left
        else:
            a, b = halves[2 * u + 1]
            totals[u * 64 : (u + 1) * 64, :] = jnp.where(low, left, turn(a) + b)

    in_cot.wait()
    total = None
    for t in range(2):
        both = dot_0(act2[:, t * 128 : (t + 1) * 128], cot_f[:, t * 512 : (t + 1) * 512])
        part = both[0:64, 0:256] + both[64:128, 256:512]
        total = part if total is None else total + part
    total = total * scale
    totals[320:384, :] = total[:, 0:128]
    totals[384:448, :] = total[:, 128:256]

    prod = dot_0(mixed[0], z[...]) * scale
    stem = None
    for r in range(4):
        part = prod[r * 64 : (r + 1) * 64, :]
        pieces = []
        for _ in range(3):
            piece = part.astype(BF16)
            pieces.append(piece)
            part = part - piece.astype(F32)
        term = dot_n(jnp.concatenate(pieces, 0), stem_places(r, True))
        term = term[0:64] + term[64:128] + term[128:192]
        stem = term if stem is None else stem + term
    totals[256:320, :] = jnp.where(low, last, stem[:, 128:256])
    totals[448:512, :] = stem[:, 0:128]
    out_copy.wait()


def unpack_kernel(totals, stem_t, conv_t, expand):
    for u in range(4):
        conv_t[:, u * 128 : (u + 1) * 128] = totals[u * 64 : (u + 1) * 64, :]
    mixed = totals[256:320, :]
    conv_t[:, 512:576] = mixed[:, 0:64]
    stem_t[:, 0:128] = totals[448:512, :]
    stem_t[:, 128:147] = turn(mixed)[:, 0:19]
    for u in range(2):
        expand[:, u * 128 : (u + 1) * 128] = totals[320 + u * 64 : 384 + u * 64, :]


def params():
    return pltpu.CompilerParams(vmem_limit_bytes=VMEM_LIMIT)


def shapes(*pairs):
    return [jax.ShapeDtypeStruct(shape, dtype) for shape, dtype in pairs]


SMEM = pl.BlockSpec(memory_space=pltpu.SMEM)
WHOLE = pl.BlockSpec(memory_space=pltpu.VMEM)
APART = pl.BlockSpec(memory_space=pl.ANY)


def prepare(tissue, cot, expand, stem_t, conv_t):
    outs = (((1024, 1024), BF16), ((1024, 256), F32), ((512, 512), BF16), ((1536, 384), BF16), ((384, 768), BF16))
    return pl.pallas_call(
        prepare_kernel,
        in_specs=[SMEM, APART, WHOLE, WHOLE, WHOLE],
        out_specs=[APART] * 5,
        out_shape=shapes(*outs),
        scratch_shapes=[pltpu.VMEM((8192, 128), BF16)]
        + [pltpu.VMEM(shape, dtype) for shape, dtype in outs]
        + [pltpu.VMEM((1024, 256), BF16), pltpu.VMEM((128, 640), F32), pltpu.SemaphoreType.DMA((15,))],
        compiler_params=params(),
        name="prepare",
    )(tissue, cot, expand, stem_t, conv_t)


def edges(tissue, cot, image, expand):
    return pl.pallas_call(
        edges_kernel,
        in_specs=[SMEM, APART, WHOLE, WHOLE],
        out_specs=[WHOLE] * 2,
        out_shape=shapes(((56, 2048), BF16), ((56, 2048), BF16)),
        scratch_shapes=[pltpu.VMEM((8192, 128), BF16), pltpu.VMEM((1024, 512), BF16), pltpu.SemaphoreType.DMA((4,))],
        compiler_params=params(),
        name="edges",
    )(tissue, cot, image, expand)


def main(tissue, own, first, second, w1, w2, back2, w2b, cot_f):
    return pl.pallas_call(
        main_kernel,
        in_specs=[SMEM] + [APART] * 8,
        out_specs=[APART, WHOLE],
        out_shape=shapes(((2048, 128), BF16), ((512, 128), F32)),
        scratch_shapes=[
            pltpu.VMEM((1, 3, 8, 2048), BF16),
            pltpu.VMEM((56, 2048), BF16),
            pltpu.VMEM((56, 2048), BF16),
            pltpu.VMEM((512, 512), BF16),
            pltpu.VMEM((1536, 384), BF16),
            pltpu.VMEM((1024, 256), F32),
            pltpu.VMEM((384, 768), BF16),
            pltpu.VMEM((1024, 1024), BF16),
            pltpu.VMEM((64, 2048), F32),
            pltpu.VMEM((1024 + 2 * PAD, 128), F32),
            pltpu.VMEM((1024, 512), BF16),
            pltpu.VMEM((1024 + 2 * PAD, 512), F32),
            pltpu.VMEM((1024, 256), F32),
            pltpu.VMEM((1024, 1152), BF16),
            pltpu.VMEM((1024, 256), BF16),
            pltpu.VMEM((1024, 384), BF16),
            pltpu.VMEM((1024 + 2 * PAD, 768), F32),
            pltpu.VMEM((2, 1024, 256), BF16),
            pltpu.VMEM((2048, 128), BF16),
            pltpu.SemaphoreType.DMA((10,)),
        ],
        compiler_params=params(),
        name="main",
    )(tissue, own, first, second, w1, w2, back2, w2b, cot_f)


def unpack(totals):
    return pl.pallas_call(
        unpack_kernel,
        in_specs=[WHOLE],
        out_specs=[WHOLE] * 3,
        out_shape=shapes(((64, 147), F32), ((64, 576), F32), ((64, 256), F32)),
        compiler_params=params(),
        name="unpack",
    )(totals)


def reduce_all(totals):
    slide = ("x", "y", "core")
    count, depth = lax.axis_size(slide), lax.axis_size("tile")
    part = lax.all_to_all(totals.reshape(count, -1, 128), slide, 0, 0, tiled=True).sum(0)
    part = lax.all_to_all(jnp.broadcast_to(part[None], (depth,) + part.shape), "tile", 0, 0, tiled=True).sum(0)
    whole = lax.all_to_all(jnp.broadcast_to(part[None], (count,) + part.shape), slide, 0, 0, tiled=True)
    return whole.reshape(totals.shape)


def per_device(image, stem_weight, conv_weight, expand_weight, cotangent, tissue):
    depth = lax.axis_size("tile")
    rows = tissue[0]
    cot = cotangent[0].reshape(4, 1024, 2, 128).transpose(1, 2, 0, 3).reshape(8192, 128)
    first, second = edges(rows, cot, image, expand_weight)
    pairs = [[(i, i + 1) for i in range(start, depth - 1, 2)] for start in (0, 1)]
    first = lax.ppermute(first, "tile", pairs[0] + [(b, a) for a, b in pairs[0]])
    second = lax.ppermute(second, "tile", pairs[1] + [(b, a) for a, b in pairs[1]])
    cot_f, back2, w1, w2, w2b = prepare(rows, cot, expand_weight, stem_weight.T, conv_weight.T)
    out, totals = main(rows, image, first, second, w1, w2, back2, w2b, cot_f)
    stem_g, conv_g, expand_g = unpack(reduce_all(totals))
    field = out.reshape(512, 4, 128).transpose(1, 0, 2)
    field = with_layout_constraint(field, Layout(major_to_minor=(1, 0, 2)))
    return field.reshape(1, 4, 65536), stem_g.T, conv_g.T, expand_g


def solution(mesh):
    slide = ("x", "y", "core")
    fine = Mesh(mesh.devices.reshape(4, 4, 2, 8), slide + ("tile",))
    placed = (P(slide, None, "tile", None), P(), P(), P(), P(slide, "tile", None), P(slide, None, None))
    return jax.shard_map(
        per_device, mesh=fine, in_specs=placed, out_specs=(P(slide, "tile", None), P(), P(), P()), check_vma=False
    )
```

```python
import jax
import jax.numpy as jnp
from jax import lax
from jax.experimental import pallas as pl
from jax.experimental.layout import Layout, with_layout_constraint
from jax.experimental.pallas import tpu as pltpu
from jax.sharding import Mesh, PartitionSpec as P

F32 = jnp.float32
BF16 = jnp.bfloat16
VMEM_LIMIT = 32 * 1024 * 1024

ROWS = (0, 1, 2, 3, -1, 4, -2, 5)
PAD = 8
CHUNKS = 8
WIDE = 128
SPAN = 256


def dot_0(left, right):
    return lax.dot_general(left, right, (((0,), (0,)), ((), ())), preferred_element_type=F32)


def dot_t(left, right):
    return lax.dot_general(left, right, (((1,), (1,)), ((), ())), preferred_element_type=F32)


def dot_n(left, right):
    return jnp.dot(left, right, preferred_element_type=F32)


def iota(shape, dim):
    return lax.broadcasted_iota(jnp.int32, shape, dim)


def lane_is_low(rows):
    return iota((rows, 128), 1) < 64


def turn(value):
    return pltpu.roll(value, 64, 1)


def sigmoid(value):
    return 1.0 / (1.0 + jnp.exp(-value))


def stem_places(row, split):
    place = iota((512, 1), 0)
    tap = place // 64
    within = place % 64
    colour = (within >= 21).astype(jnp.int32) + (within >= 42).astype(jnp.int32)
    line = within - 21 * colour - (2 * row + 4)
    valid = (tap >= 1) & (within < 63) & (line >= 0) & (line <= 6)
    entry = line * 21 + (tap - 1) * 3 + colour
    if split:
        entry = jnp.where(entry < 128, entry, entry + 64)
    entry = jnp.where(valid, entry, -1)
    return (iota((512, 256), 1) == entry).astype(F32).astype(BF16)


def is_even():
    return lax.axis_index("tile") % 2 == 0


def fetcher(sems):
    count = [0]

    def fetch(src, dst):
        copy = pltpu.make_async_copy(src, dst, sems.at[count[0]])
        copy.start()
        count[0] += 1
        return copy

    return fetch


def edges_kernel(tissue, cot_i, image_i, expand_i, to_first, to_second, cot, image, expand, rows, sems):
    even = is_even()
    fetch = fetcher(sems)
    in_expand = fetch(expand_i, expand)
    parts = [fetch(cot_i.at[pl.ds(q * 2048, 2048)], cot.at[pl.ds(q * 2048, 2048)]) for q in range(4)]
    in_image = fetch(image_i, image)
    m, k = iota((128, 256), 0), iota((128, 256), 1)
    source = (m % 32) * 8 + ((m // 32) % 2) * 4 + (m // 64) * 3
    order = (k == source).astype(F32).astype(BF16)
    in_expand.wait()
    both = jnp.concatenate([expand[...].astype(F32)] * 2, 0).T
    low = lane_is_low(256)
    wide = jnp.concatenate([jnp.where(low, both, 0.0), jnp.where(low, 0.0, both)], 0).astype(BF16)
    low = lane_is_low(128)
    for q in range(4):
        parts[q].wait()
        for s in range(8):
            got = dot_n(order, cot[q * 2048 + s * 256 : q * 2048 + (s + 1) * 256, :]).astype(BF16)
            for n in range(4):
                rows[q * 256 + s * 32 : q * 256 + (s + 1) * 32, n * 128 : (n + 1) * 128] = got[n * 32 : (n + 1) * 32, :]
        back = dot_n(rows[q * 256 : (q + 1) * 256, :], wide) * tissue[0, q].astype(F32)
        a, b = back[0:128], back[128:256]
        top = jnp.where(low, a, turn(b))
        bottom = jnp.where(low, turn(a), b)
        first = jnp.where(even, bottom, top).astype(BF16)
        second = jnp.where(even, top, bottom).astype(BF16)
        for v in range(4):
            u = q * 4 + v
            to_first[0:32, u * 128 : (u + 1) * 128] = first[v * 32 : (v + 1) * 32, :]
            to_second[0:32, u * 128 : (u + 1) * 128] = second[v * 32 : (v + 1) * 32, :]
    in_image.wait()
    for k in range(3):
        to_first[32 + 8 * k : 40 + 8 * k, :] = image[0, k]
        to_second[32 + 8 * k : 40 + 8 * k, :] = image[0, k]


def prepare_kernel(tissue, cot_i, expand, stem_t, conv_t, cot_f, back2, w1, w2, w2b, cot, wide, filt, sems):
    fetch = fetcher(sems)
    parts = [fetch(cot_i.at[pl.ds(q * 2048, 2048)], cot.at[pl.ds(q * 2048, 2048)]) for q in range(4)]

    filt[...] = jnp.zeros(filt.shape, F32)
    filt[0:64, 0:147] = stem_t[...].astype(F32)
    both = filt[0:64, 0:256]
    both = jnp.concatenate([both, both], 0).T
    low = lane_is_low(256)
    halves = [jnp.where(low, both, 0.0).astype(BF16), jnp.where(low, 0.0, both).astype(BF16)]
    for t in range(4):
        tile = dot_n(stem_places(ROWS[2 * t], False), halves[0]) + dot_n(stem_places(ROWS[2 * t + 1], False), halves[1])
        w1[:, t * 128 : (t + 1) * 128] = tile.astype(BF16)

    filt[0:64, 0:576] = conv_t[...].astype(F32)
    filt[64:128, 0:576] = conv_t[...].astype(F32)
    turned = filt[...].T
    low = lane_is_low(64)
    flat = jnp.zeros((64, 128), F32)

    def pair(i0, i1, j):
        tiles = [turned[(3 * i + j) * 64 : (3 * i + j + 1) * 64, :] if 0 <= i <= 2 else flat for i in (i0, i1)]
        return jnp.where(low, tiles[0], tiles[1]).astype(BF16)

    for j in range(3):
        for a in range(8):
            base = j * 384 + a * 64 if a < 6 else 1152 + j * 128 + (a - 6) * 64
            for t in range(3):
                i0, i1 = (ROWS[a] - ROWS[2 * t + e] + 1 for e in range(2))
                w2[base : base + 64, t * 128 : (t + 1) * 128] = pair(i0, i1, j)
    blocks = [conv_t[:, n * 64 : (n + 1) * 64].astype(F32) for n in range(9)]
    empty = jnp.zeros((64, 64), F32)

    def block(i, j):
        return blocks[3 * i + j] if 0 <= i <= 2 else empty

    for j in range(3):
        for slot in range(6):
            for t in range(2):
                tile = jnp.concatenate([block(2 * t + e - ROWS[slot] + 1, j) for e in range(2)], 1)
                w2b[slot * 64 : (slot + 1) * 64, j * 256 + t * 128 : j * 256 + (t + 1) * 128] = tile.astype(BF16)

    m, k = iota((256, 256), 0), iota((256, 256), 1)
    source = (m % 32) * 8 + ((m // 32) % 2) * 4 + m // 64
    order = (k == source).astype(F32).astype(BF16)
    wide[...] = jnp.zeros(wide.shape, BF16)
    both = jnp.concatenate([expand[...].astype(F32)] * 2, 0).T
    low = lane_is_low(256)
    for r in range(4):
        keep = low if r % 2 == 0 else jnp.logical_not(low)
        wide[r * 256 : (r + 1) * 256, (r // 2) * 128 : (r // 2 + 1) * 128] = jnp.where(keep, both, 0.0).astype(BF16)
    for q in range(4):
        parts[q].wait()
        for s in range(8):
            got = dot_n(order, cot[q * 2048 + s * 256 : q * 2048 + (s + 1) * 256, :]).astype(BF16)
            for n in range(8):
                cot_f[q * 256 + s * 32 : q * 256 + (s + 1) * 32, n * 128 : (n + 1) * 128] = got[n * 32 : (n + 1) * 32, :]
        part = pl.ds(q * 256, 256)
        back2[part, :] = dot_n(cot_f[part, :], wide[...]) * tissue[0, q].astype(F32)


def main_kernel(
    tissue, own, first, second, w1, w2, back2, w2b, cot_f, out_o, totals,
    lines, cols, z, act, slope1, act_sh, act2, grad2, wide, mixed, out, sems,
):
    fetch = fetcher(sems)
    even = is_even()

    def received(rows, lanes):
        a, b = first[rows, lanes].astype(F32), second[rows, lanes].astype(F32)
        return jnp.where(even, b, a), jnp.where(even, a, b)

    m, x = iota((128, 512), 0), iota((128, 512), 1)
    pick = (x == jnp.where(x < 256, 2 * m, 2 * m + 257)).astype(F32).astype(BF16)
    cols[0:PAD, :] = jnp.zeros((PAD, 128), F32)
    cols[PAD + 1024 :, :] = jnp.zeros((PAD, 128), F32)
    act[0:PAD, :] = jnp.zeros((PAD, 512), F32)
    act[PAD + 1024 :, :] = jnp.zeros((PAD, 512), F32)
    wide[0:PAD, :] = jnp.zeros((PAD, 768), F32)
    wide[PAD + 1024 :, :] = jnp.zeros((PAD, 768), F32)
    lines[63:64, :] = jnp.zeros((1, 2048), F32)
    none = jnp.zeros((64, 256), BF16)
    for k in range(3):
        before, after = received(slice(32 + 8 * k, 40 + 8 * k), slice(None))
        lines[21 * k : 21 * k + 7, :] = before[1:8]
        lines[21 * k + 7 : 21 * k + 15, :] = own[0, k].astype(F32)
        lines[21 * k + 15 : 21 * k + 21, :] = after[0:6]
    for t in range(8):
        part = lines[:, t * 256 : (t + 1) * 256].astype(BF16)
        spread = jnp.concatenate([jnp.concatenate([part, none], 0), jnp.concatenate([none, part], 0)], 1)
        cols[PAD + t * 128 : PAD + (t + 1) * 128, :] = dot_t(pick, spread)

    position = lax.axis_index("tile")
    ends = jnp.where(lane_is_low(1), (position > 0).astype(F32), (position < lax.axis_size("tile") - 1).astype(F32))
    for t in range(CHUNKS):
        at = t * WIDE
        wins = [cols[PAD + at + s : PAD + at + s + WIDE, :].astype(BF16) for s in (-2, -1, 0, 1)]
        zt = jnp.concatenate(wins, 1)
        z[at : at + WIDE, :] = zt
        pre = dot_n(zt, w1[...])
        sig = sigmoid(pre)
        value = pre * sig
        act[PAD + at : PAD + at + WIDE, 0:256] = value[:, :256]
        act[PAD + at : PAD + at + WIDE, 256:384] = value[:, 256:384] * ends
        act[PAD + at : PAD + at + WIDE, 384:512] = value[:, 384:512] * ends
        slope1[at : at + WIDE, :] = (sig * (1.0 + pre * (1.0 - sig)))[:, :256]

    low = lane_is_low(128)
    for t in range(1024 // SPAN):
        at = t * SPAN
        wins = [act[PAD + at + j - 1 : PAD + at + j - 1 + SPAN, :].astype(BF16) for j in range(3)]
        near = jnp.concatenate([win[:, :384] for win in wins], 1)
        act_sh[at : at + SPAN, :] = near
        pre = dot_n(near, w2[0:1152, 0:256])
        sig = sigmoid(pre)
        keep = tissue[0, at // 256].astype(F32)
        act2[at : at + SPAN, :] = (pre * sig * keep).astype(BF16)
        grad2[at : at + SPAN, 0:256] = (back2[at : at + SPAN, :] * (sig * (1.0 + pre * (1.0 - sig)))).astype(BF16)
        pre = dot_n(jnp.concatenate([near] + [win[:, 384:] for win in wins], 1), w2[:, 256:384])
        sig = sigmoid(pre)
        ends = []
        for u in range(at // 128, (at + SPAN) // 128):
            tiles = [received(slice(0, 32), slice(v * 128, (v + 1) * 128)) for v in range((u // 2) * 4, (u // 2) * 4 + 4)]
            a, b = (jnp.concatenate(half, 0) for half in zip(*tiles))
            ends.append(jnp.where(low, turn(a), b) if u % 2 else jnp.where(low, a, turn(b)))
        slope = sig * (1.0 + pre * (1.0 - sig))
        grad2[at : at + SPAN, 256:384] = (jnp.concatenate(ends, 0) * slope).astype(BF16)
        wide[PAD + at : PAD + at + SPAN, :] = dot_n(grad2[at : at + SPAN, :], w2b[...])

    for t in range(CHUNKS):
        at = t * WIDE
        back = wide[PAD + at + 1 : PAD + at + 1 + WIDE, 0:256] + wide[PAD + at : PAD + at + WIDE, 256:512]
        back = back + wide[PAD + at - 1 : PAD + at - 1 + WIDE, 512:768]
        gb = (back * slope1[at : at + WIDE, :]).astype(BF16)
        mixed[0, at : at + WIDE, :] = gb
        gr = gb.astype(F32)
        mixed[1, at : at + WIDE, :] = jnp.concatenate([turn(gr[:, :128]), turn(gr[:, 128:])], 1).astype(BF16)

    n, k = iota((256, 256), 0), iota((256, 256), 1)
    odd, r, two = n // 128, n % 4, (n % 128) // 4
    source = (r // 2) * 128 + ((r + odd) % 2) * 64 + 2 * two + odd
    order = (k == source).astype(F32).astype(BF16)
    for t in range(8):
        stacks = []
        for at in (t * 128, t * 128 + 64):
            stacks.append(jnp.concatenate([mixed[v, at : at + 64, u * 128 : (u + 1) * 128] for u in range(2) for v in range(2)], 0))
        got = dot_n(order, jnp.concatenate(stacks, 1))
        for e in range(2):
            at = t * 256 + e * 128
            out[at : at + 128, :] = jnp.where(low, got[0:128, e * 128 : e * 128 + 128], got[128:256, e * 128 : e * 128 + 128]).astype(BF16)
    out_copy = fetch(out, out_o)

    scale = 1.0 / 1024.0
    low = lane_is_low(64)
    prod = dot_0(grad2[:, 0:256], act_sh[...]) * scale
    halves = {}
    for i in range(3):
        for j in range(3):
            at_low, at_high = [], []
            for r in range(4):
                slot = ROWS.index(r + i - 1)
                col = j * 384 + (slot // 2) * 128
                tile = prod[r * 64 : (r + 1) * 64, col : col + 128]
                (at_high if slot % 2 else at_low).append(tile)
            halves[3 * i + j] = (sum(at_low[1:], at_low[0]), sum(at_high[1:], at_high[0]))
    last = None
    for u in range(5):
        a, b = halves[2 * u]
        left = a + turn(b)
        if u == 4:
            last = left
        else:
            a, b = halves[2 * u + 1]
            totals[u * 64 : (u + 1) * 64, :] = jnp.where(low, left, turn(a) + b)

    total = None
    for t in range(2):
        both = dot_0(act2[:, t * 128 : (t + 1) * 128], cot_f[:, t * 512 : (t + 1) * 512])
        part = both[0:64, 0:256] + both[64:128, 256:512]
        total = part if total is None else total + part
    total = total * scale
    totals[320:384, :] = total[:, 0:128]
    totals[384:448, :] = total[:, 128:256]

    prod = dot_0(mixed[0], z[...]) * scale
    stem = None
    for r in range(4):
        part = prod[r * 64 : (r + 1) * 64, :]
        pieces = []
        for _ in range(3):
            piece = part.astype(BF16)
            pieces.append(piece)
            part = part - piece.astype(F32)
        term = dot_n(jnp.concatenate(pieces, 0), stem_places(r, True))
        term = term[0:64] + term[64:128] + term[128:192]
        stem = term if stem is None else stem + term
    totals[256:320, :] = jnp.where(low, last, stem[:, 128:256])
    totals[448:512, :] = stem[:, 0:128]
    out_copy.wait()


def unpack_kernel(totals, stem_t, conv_t, expand):
    for u in range(4):
        conv_t[:, u * 128 : (u + 1) * 128] = totals[u * 64 : (u + 1) * 64, :]
    mixed = totals[256:320, :]
    conv_t[:, 512:576] = mixed[:, 0:64]
    stem_t[:, 0:128] = totals[448:512, :]
    stem_t[:, 128:147] = turn(mixed)[:, 0:19]
    for u in range(2):
        expand[:, u * 128 : (u + 1) * 128] = totals[320 + u * 64 : 384 + u * 64, :]


def params():
    return pltpu.CompilerParams(vmem_limit_bytes=VMEM_LIMIT)


def shapes(*pairs):
    return [jax.ShapeDtypeStruct(shape, dtype) for shape, dtype in pairs]


def near(value):
    return pltpu.with_memory_space_constraint(value, pltpu.VMEM)


def far(value):
    return pltpu.with_memory_space_constraint(value, pltpu.HBM)


SMEM = pl.BlockSpec(memory_space=pltpu.SMEM)
WHOLE = pl.BlockSpec(memory_space=pltpu.VMEM)
APART = pl.BlockSpec(memory_space=pl.ANY)


def prepare(tissue, cot, expand, stem_t, conv_t):
    outs = (((1024, 1024), BF16), ((1024, 256), F32), ((512, 512), BF16), ((1536, 384), BF16), ((384, 768), BF16))
    return pl.pallas_call(
        prepare_kernel,
        in_specs=[SMEM, APART, WHOLE, WHOLE, WHOLE],
        out_specs=[WHOLE] * 5,
        out_shape=[pltpu.VMEM(shape, dtype) for shape, dtype in outs],
        scratch_shapes=[
            pltpu.VMEM((8192, 128), BF16),
            pltpu.VMEM((1024, 256), BF16),
            pltpu.VMEM((128, 640), F32),
            pltpu.SemaphoreType.DMA((4,)),
        ],
        compiler_params=params(),
        name="prepare",
    )(far(tissue), far(cot), expand, stem_t, conv_t)


def edges(tissue, cot, image, expand):
    return pl.pallas_call(
        edges_kernel,
        in_specs=[SMEM, APART, APART, APART],
        out_specs=[WHOLE] * 2,
        out_shape=[pltpu.VMEM((56, 2048), BF16)] * 2,
        scratch_shapes=[
            pltpu.VMEM((8192, 128), BF16),
            pltpu.VMEM((1, 3, 8, 2048), BF16),
            pltpu.VMEM((64, 256), BF16),
            pltpu.VMEM((1024, 512), BF16),
            pltpu.SemaphoreType.DMA((6,)),
        ],
        compiler_params=params(),
        name="edges",
    )(far(tissue), far(cot), far(image), far(expand))


def main(tissue, *others):
    return pl.pallas_call(
        main_kernel,
        in_specs=[SMEM] + [WHOLE] * 8,
        out_specs=[APART, WHOLE],
        out_shape=[jax.ShapeDtypeStruct((2048, 128), BF16), pltpu.VMEM((512, 128), F32)],
        scratch_shapes=[
            pltpu.VMEM((64, 2048), F32),
            pltpu.VMEM((1024 + 2 * PAD, 128), F32),
            pltpu.VMEM((1024, 512), BF16),
            pltpu.VMEM((1024 + 2 * PAD, 512), F32),
            pltpu.VMEM((1024, 256), F32),
            pltpu.VMEM((1024, 1152), BF16),
            pltpu.VMEM((1024, 256), BF16),
            pltpu.VMEM((1024, 384), BF16),
            pltpu.VMEM((1024 + 2 * PAD, 768), F32),
            pltpu.VMEM((2, 1024, 256), BF16),
            pltpu.VMEM((2048, 128), BF16),
            pltpu.SemaphoreType.DMA((2,)),
        ],
        compiler_params=params(),
        name="main",
    )(far(tissue), *map(near, others))


def unpack(totals):
    return pl.pallas_call(
        unpack_kernel,
        in_specs=[WHOLE],
        out_specs=[WHOLE] * 3,
        out_shape=shapes(((64, 147), F32), ((64, 576), F32), ((64, 256), F32)),
        compiler_params=params(),
        name="unpack",
    )(near(totals))


def reduce_all(totals):
    slide = ("x", "y", "core")
    count, depth = lax.axis_size(slide), lax.axis_size("tile")
    part = lax.all_to_all(totals.reshape(count, -1, 128), slide, 0, 0, tiled=True).sum(0)
    part = lax.all_to_all(jnp.broadcast_to(part[None], (depth,) + part.shape), "tile", 0, 0, tiled=True).sum(0)
    whole = lax.all_to_all(jnp.broadcast_to(part[None], (count,) + part.shape), slide, 0, 0, tiled=True)
    return whole.reshape(totals.shape)


def per_device(image, stem_weight, conv_weight, expand_weight, cotangent, tissue):
    depth = lax.axis_size("tile")
    rows = tissue[0]
    cot = cotangent[0].reshape(4, 1024, 2, 128).transpose(1, 2, 0, 3).reshape(8192, 128)
    first, second = edges(rows, cot, image, expand_weight)
    pairs = [[(i, i + 1) for i in range(start, depth - 1, 2)] for start in (0, 1)]
    first = lax.ppermute(first, "tile", pairs[0] + [(b, a) for a, b in pairs[0]])
    second = lax.ppermute(second, "tile", pairs[1] + [(b, a) for a, b in pairs[1]])
    cot_f, back2, w1, w2, w2b = prepare(rows, cot, expand_weight, stem_weight.T, conv_weight.T)
    out, totals = main(rows, image, first, second, w1, w2, back2, w2b, cot_f)
    stem_g, conv_g, expand_g = unpack(reduce_all(totals))
    field = out.reshape(512, 4, 128).transpose(1, 0, 2)
    field = with_layout_constraint(field, Layout(major_to_minor=(1, 0, 2)))
    return field.reshape(1, 4, 65536), stem_g.T, conv_g.T, expand_g


def solution(mesh):
    slide = ("x", "y", "core")
    fine = Mesh(mesh.devices.reshape(4, 4, 2, 8), slide + ("tile",))
    placed = (P(slide, None, "tile", None), P(), P(), P(), P(slide, "tile", None), P(slide, None, None))
    return jax.shard_map(
        per_device, mesh=fine, in_specs=placed, out_specs=(P(slide, "tile", None), P(), P(), P()), check_vma=False
    )
```

```python
import jax
import jax.numpy as jnp
from jax import lax
from jax.experimental import pallas as pl
from jax.experimental.layout import Layout, with_layout_constraint
from jax.experimental.pallas import tpu as pltpu
from jax.sharding import Mesh, PartitionSpec as P

F32 = jnp.float32
BF16 = jnp.bfloat16
VMEM_LIMIT = 32 * 1024 * 1024

ROWS = (0, 1, 2, 3, -1, 4, -2, 5)
PAD = 8
CHUNKS = 8
WIDE = 128
SPAN = 256


def dot_0(left, right):
    return lax.dot_general(left, right, (((0,), (0,)), ((), ())), preferred_element_type=F32)


def dot_t(left, right):
    return lax.dot_general(left, right, (((1,), (1,)), ((), ())), preferred_element_type=F32)


def dot_n(left, right):
    return jnp.dot(left, right, preferred_element_type=F32)


def iota(shape, dim):
    return lax.broadcasted_iota(jnp.int32, shape, dim)


def lane_is_low(rows):
    return iota((rows, 128), 1) < 64


def turn(value):
    return pltpu.roll(value, 64, 1)


def sigmoid(value):
    return 1.0 / (1.0 + jnp.exp(-value))


def stem_places(row, split):
    place = iota((512, 1), 0)
    tap = place // 64
    within = place % 64
    colour = (within >= 21).astype(jnp.int32) + (within >= 42).astype(jnp.int32)
    line = within - 21 * colour - (2 * row + 4)
    valid = (tap >= 1) & (within < 63) & (line >= 0) & (line <= 6)
    entry = line * 21 + (tap - 1) * 3 + colour
    if split:
        entry = jnp.where(entry < 128, entry, entry + 64)
    entry = jnp.where(valid, entry, -1)
    return (iota((512, 256), 1) == entry).astype(F32).astype(BF16)


def is_even():
    return lax.axis_index("tile") % 2 == 0


def fetcher(sems):
    count = [0]

    def fetch(src, dst):
        copy = pltpu.make_async_copy(src, dst, sems.at[count[0]])
        copy.start()
        count[0] += 1
        return copy

    return fetch


def edges_kernel(tissue, cot_i, image_i, expand_i, to_first, to_second, cot, image, expand, rows, sems):
    even = is_even()
    fetch = fetcher(sems)
    in_expand = fetch(expand_i, expand)
    parts = [fetch(cot_i.at[pl.ds(q * 2048, 2048)], cot.at[pl.ds(q * 2048, 2048)]) for q in range(4)]
    in_image = fetch(image_i, image)
    m, k = iota((128, 256), 0), iota((128, 256), 1)
    source = (m % 32) * 8 + ((m // 32) % 2) * 4 + (m // 64) * 3
    order = (k == source).astype(F32).astype(BF16)
    in_expand.wait()
    both = jnp.concatenate([expand[...].astype(F32)] * 2, 0).T
    low = lane_is_low(256)
    wide = jnp.concatenate([jnp.where(low, both, 0.0), jnp.where(low, 0.0, both)], 0).astype(BF16)
    low = lane_is_low(128)
    for part in parts:
        part.wait()
    for q in range(4):
        for s in range(8):
            got = dot_n(order, cot[q * 2048 + s * 256 : q * 2048 + (s + 1) * 256, :]).astype(BF16)
            for n in range(4):
                rows[q * 256 + s * 32 : q * 256 + (s + 1) * 32, n * 128 : (n + 1) * 128] = got[n * 32 : (n + 1) * 32, :]
        back = dot_n(rows[q * 256 : (q + 1) * 256, :], wide) * tissue[0, q].astype(F32)
        a, b = back[0:128], back[128:256]
        top = jnp.where(low, a, turn(b))
        bottom = jnp.where(low, turn(a), b)
        first = jnp.where(even, bottom, top).astype(BF16)
        second = jnp.where(even, top, bottom).astype(BF16)
        for v in range(4):
            u = q * 4 + v
            to_first[0:32, u * 128 : (u + 1) * 128] = first[v * 32 : (v + 1) * 32, :]
            to_second[0:32, u * 128 : (u + 1) * 128] = second[v * 32 : (v + 1) * 32, :]
    in_image.wait()
    for k in range(3):
        to_first[32 + 8 * k : 40 + 8 * k, :] = image[0, k]
        to_second[32 + 8 * k : 40 + 8 * k, :] = image[0, k]


def prepare_kernel(tissue, cot_i, expand, stem_t, conv_t, cot_f, back2, w1, w2, w2b, cot, wide, filt, sems):
    fetch = fetcher(sems)
    parts = [fetch(cot_i.at[pl.ds(q * 2048, 2048)], cot.at[pl.ds(q * 2048, 2048)]) for q in range(4)]

    filt[...] = jnp.zeros(filt.shape, F32)
    filt[0:64, 0:147] = stem_t[...].astype(F32)
    both = filt[0:64, 0:256]
    both = jnp.concatenate([both, both], 0).T
    low = lane_is_low(256)
    halves = [jnp.where(low, both, 0.0).astype(BF16), jnp.where(low, 0.0, both).astype(BF16)]
    for t in range(4):
        tile = dot_n(stem_places(ROWS[2 * t], False), halves[0]) + dot_n(stem_places(ROWS[2 * t + 1], False), halves[1])
        w1[:, t * 128 : (t + 1) * 128] = tile.astype(BF16)

    filt[0:64, 0:576] = conv_t[...].astype(F32)
    filt[64:128, 0:576] = conv_t[...].astype(F32)
    turned = filt[...].T
    low = lane_is_low(64)
    flat = jnp.zeros((64, 128), F32)

    def pair(i0, i1, j):
        tiles = [turned[(3 * i + j) * 64 : (3 * i + j + 1) * 64, :] if 0 <= i <= 2 else flat for i in (i0, i1)]
        return jnp.where(low, tiles[0], tiles[1]).astype(BF16)

    for j in range(3):
        for a in range(8):
            base = j * 384 + a * 64 if a < 6 else 1152 + j * 128 + (a - 6) * 64
            for t in range(3):
                i0, i1 = (ROWS[a] - ROWS[2 * t + e] + 1 for e in range(2))
                w2[base : base + 64, t * 128 : (t + 1) * 128] = pair(i0, i1, j)
    blocks = [conv_t[:, n * 64 : (n + 1) * 64].astype(F32) for n in range(9)]
    empty = jnp.zeros((64, 64), F32)

    def block(i, j):
        return blocks[3 * i + j] if 0 <= i <= 2 else empty

    for j in range(3):
        for slot in range(6):
            for t in range(2):
                tile = jnp.concatenate([block(2 * t + e - ROWS[slot] + 1, j) for e in range(2)], 1)
                w2b[slot * 64 : (slot + 1) * 64, j * 256 + t * 128 : j * 256 + (t + 1) * 128] = tile.astype(BF16)

    m, k = iota((256, 256), 0), iota((256, 256), 1)
    source = (m % 32) * 8 + ((m // 32) % 2) * 4 + m // 64
    order = (k == source).astype(F32).astype(BF16)
    wide[...] = jnp.zeros(wide.shape, BF16)
    both = jnp.concatenate([expand[...].astype(F32)] * 2, 0).T
    low = lane_is_low(256)
    for r in range(4):
        keep = low if r % 2 == 0 else jnp.logical_not(low)
        wide[r * 256 : (r + 1) * 256, (r // 2) * 128 : (r // 2 + 1) * 128] = jnp.where(keep, both, 0.0).astype(BF16)
    for q in range(4):
        parts[q].wait()
        for s in range(8):
            got = dot_n(order, cot[q * 2048 + s * 256 : q * 2048 + (s + 1) * 256, :]).astype(BF16)
            for n in range(8):
                cot_f[q * 256 + s * 32 : q * 256 + (s + 1) * 32, n * 128 : (n + 1) * 128] = got[n * 32 : (n + 1) * 32, :]
        part = pl.ds(q * 256, 256)
        back2[part, :] = dot_n(cot_f[part, :], wide[...]) * tissue[0, q].astype(F32)


def main_kernel(
    tissue, own, first, second, w1, w2, back2, w2b, cot_f, out_o, totals,
    lines, cols, z, act, slope1, act_sh, act2, grad2, wide, mixed, out, sems,
):
    fetch = fetcher(sems)
    even = is_even()

    def received(rows, lanes):
        a, b = first[rows, lanes].astype(F32), second[rows, lanes].astype(F32)
        return jnp.where(even, b, a), jnp.where(even, a, b)

    m, x = iota((128, 512), 0), iota((128, 512), 1)
    pick = (x == jnp.where(x < 256, 2 * m, 2 * m + 257)).astype(F32).astype(BF16)
    cols[0:PAD, :] = jnp.zeros((PAD, 128), F32)
    cols[PAD + 1024 :, :] = jnp.zeros((PAD, 128), F32)
    act[0:PAD, :] = jnp.zeros((PAD, 512), F32)
    act[PAD + 1024 :, :] = jnp.zeros((PAD, 512), F32)
    wide[0:PAD, :] = jnp.zeros((PAD, 768), F32)
    wide[PAD + 1024 :, :] = jnp.zeros((PAD, 768), F32)
    lines[63:64, :] = jnp.zeros((1, 2048), F32)
    none = jnp.zeros((64, 256), BF16)
    for k in range(3):
        before, after = received(slice(32 + 8 * k, 40 + 8 * k), slice(None))
        lines[21 * k : 21 * k + 7, :] = before[1:8]
        lines[21 * k + 7 : 21 * k + 15, :] = own[0, k].astype(F32)
        lines[21 * k + 15 : 21 * k + 21, :] = after[0:6]
    for t in range(8):
        part = lines[:, t * 256 : (t + 1) * 256].astype(BF16)
        spread = jnp.concatenate([jnp.concatenate([part, none], 0), jnp.concatenate([none, part], 0)], 1)
        cols[PAD + t * 128 : PAD + (t + 1) * 128, :] = dot_t(pick, spread)

    position = lax.axis_index("tile")
    ends = jnp.where(lane_is_low(1), (position > 0).astype(F32), (position < lax.axis_size("tile") - 1).astype(F32))
    for t in range(CHUNKS):
        at = t * WIDE
        wins = [cols[PAD + at + s : PAD + at + s + WIDE, :].astype(BF16) for s in (-2, -1, 0, 1)]
        zt = jnp.concatenate(wins, 1)
        z[at : at + WIDE, :] = zt
        pre = dot_n(zt, w1[...])
        sig = sigmoid(pre)
        value = pre * sig
        act[PAD + at : PAD + at + WIDE, 0:256] = value[:, :256]
        act[PAD + at : PAD + at + WIDE, 256:384] = value[:, 256:384] * ends
        act[PAD + at : PAD + at + WIDE, 384:512] = value[:, 384:512] * ends
        slope1[at : at + WIDE, :] = (sig * (1.0 + pre * (1.0 - sig)))[:, :256]

    low = lane_is_low(128)
    for t in range(1024 // SPAN):
        at = t * SPAN
        wins = [act[PAD + at + j - 1 : PAD + at + j - 1 + SPAN, :].astype(BF16) for j in range(3)]
        near = jnp.concatenate([win[:, :384] for win in wins], 1)
        act_sh[at : at + SPAN, :] = near
        pre = dot_n(near, w2[0:1152, 0:256])
        sig = sigmoid(pre)
        keep = tissue[0, at // 256].astype(F32)
        act2[at : at + SPAN, :] = (pre * sig * keep).astype(BF16)
        grad2[at : at + SPAN, 0:256] = (back2[at : at + SPAN, :] * (sig * (1.0 + pre * (1.0 - sig)))).astype(BF16)
        pre = dot_n(jnp.concatenate([near] + [win[:, 384:] for win in wins], 1), w2[:, 256:384])
        sig = sigmoid(pre)
        ends = []
        for u in range(at // 128, (at + SPAN) // 128):
            tiles = [received(slice(0, 32), slice(v * 128, (v + 1) * 128)) for v in range((u // 2) * 4, (u // 2) * 4 + 4)]
            a, b = (jnp.concatenate(half, 0) for half in zip(*tiles))
            ends.append(jnp.where(low, turn(a), b) if u % 2 else jnp.where(low, a, turn(b)))
        slope = sig * (1.0 + pre * (1.0 - sig))
        grad2[at : at + SPAN, 256:384] = (jnp.concatenate(ends, 0) * slope).astype(BF16)
        wide[PAD + at : PAD + at + SPAN, :] = dot_n(grad2[at : at + SPAN, :], w2b[...])

    for t in range(CHUNKS):
        at = t * WIDE
        back = wide[PAD + at + 1 : PAD + at + 1 + WIDE, 0:256] + wide[PAD + at : PAD + at + WIDE, 256:512]
        back = back + wide[PAD + at - 1 : PAD + at - 1 + WIDE, 512:768]
        gb = (back * slope1[at : at + WIDE, :]).astype(BF16)
        mixed[0, at : at + WIDE, :] = gb
        gr = gb.astype(F32)
        mixed[1, at : at + WIDE, :] = jnp.concatenate([turn(gr[:, :128]), turn(gr[:, 128:])], 1).astype(BF16)

    n, k = iota((256, 256), 0), iota((256, 256), 1)
    odd, r, two = n // 128, n % 4, (n % 128) // 4
    source = (r // 2) * 128 + ((r + odd) % 2) * 64 + 2 * two + odd
    order = (k == source).astype(F32).astype(BF16)
    for t in range(8):
        stacks = []
        for at in (t * 128, t * 128 + 64):
            stacks.append(jnp.concatenate([mixed[v, at : at + 64, u * 128 : (u + 1) * 128] for u in range(2) for v in range(2)], 0))
        got = dot_n(order, jnp.concatenate(stacks, 1))
        for e in range(2):
            at = t * 256 + e * 128
            out[at : at + 128, :] = jnp.where(low, got[0:128, e * 128 : e * 128 + 128], got[128:256, e * 128 : e * 128 + 128]).astype(BF16)
    out_copy = fetch(out, out_o)

    scale = 1.0 / 1024.0
    low = lane_is_low(64)
    prod = dot_0(grad2[:, 0:256], act_sh[...]) * scale
    halves = {}
    for i in range(3):
        for j in range(3):
            at_low, at_high = [], []
            for r in range(4):
                slot = ROWS.index(r + i - 1)
                col = j * 384 + (slot // 2) * 128
                tile = prod[r * 64 : (r + 1) * 64, col : col + 128]
                (at_high if slot % 2 else at_low).append(tile)
            halves[3 * i + j] = (sum(at_low[1:], at_low[0]), sum(at_high[1:], at_high[0]))
    last = None
    for u in range(5):
        a, b = halves[2 * u]
        left = a + turn(b)
        if u == 4:
            last = left
        else:
            a, b = halves[2 * u + 1]
            totals[u * 64 : (u + 1) * 64, :] = jnp.where(low, left, turn(a) + b)

    total = None
    for t in range(2):
        both = dot_0(act2[:, t * 128 : (t + 1) * 128], cot_f[:, t * 512 : (t + 1) * 512])
        part = both[0:64, 0:256] + both[64:128, 256:512]
        total = part if total is None else total + part
    total = total * scale
    totals[320:384, :] = total[:, 0:128]
    totals[384:448, :] = total[:, 128:256]

    prod = dot_0(mixed[0], z[...]) * scale
    stem = None
    for r in range(4):
        part = prod[r * 64 : (r + 1) * 64, :]
        pieces = []
        for _ in range(3):
            piece = part.astype(BF16)
            pieces.append(piece)
            part = part - piece.astype(F32)
        term = dot_n(jnp.concatenate(pieces, 0), stem_places(r, True))
        term = term[0:64] + term[64:128] + term[128:192]
        stem = term if stem is None else stem + term
    totals[256:320, :] = jnp.where(low, last, stem[:, 128:256])
    totals[448:512, :] = stem[:, 0:128]
    out_copy.wait()


def unpack_kernel(totals, stem_t, conv_t, expand):
    for u in range(4):
        conv_t[:, u * 128 : (u + 1) * 128] = totals[u * 64 : (u + 1) * 64, :].astype(F32)
    mixed = totals[256:320, :].astype(F32)
    conv_t[:, 512:576] = mixed[:, 0:64]
    stem_t[:, 0:128] = totals[448:512, :].astype(F32)
    stem_t[:, 128:147] = turn(mixed)[:, 0:19]
    for u in range(2):
        expand[:, u * 128 : (u + 1) * 128] = totals[320 + u * 64 : 384 + u * 64, :].astype(F32)


def params():
    return pltpu.CompilerParams(vmem_limit_bytes=VMEM_LIMIT)


def shapes(*pairs):
    return [jax.ShapeDtypeStruct(shape, dtype) for shape, dtype in pairs]


def near(value):
    return pltpu.with_memory_space_constraint(value, pltpu.VMEM)


def far(value):
    return pltpu.with_memory_space_constraint(value, pltpu.HBM)


SMEM = pl.BlockSpec(memory_space=pltpu.SMEM)
WHOLE = pl.BlockSpec(memory_space=pltpu.VMEM)
APART = pl.BlockSpec(memory_space=pl.ANY)


def prepare(tissue, cot, expand, stem_t, conv_t):
    outs = (((1024, 1024), BF16), ((1024, 256), F32), ((512, 512), BF16), ((1536, 384), BF16), ((384, 768), BF16))
    return pl.pallas_call(
        prepare_kernel,
        in_specs=[SMEM, APART, WHOLE, WHOLE, WHOLE],
        out_specs=[WHOLE] * 5,
        out_shape=[pltpu.VMEM(shape, dtype) for shape, dtype in outs],
        scratch_shapes=[
            pltpu.VMEM((8192, 128), BF16),
            pltpu.VMEM((1024, 256), BF16),
            pltpu.VMEM((128, 640), F32),
            pltpu.SemaphoreType.DMA((4,)),
        ],
        compiler_params=params(),
        name="prepare",
    )(far(tissue), far(cot), expand, stem_t, conv_t)


def edges(tissue, cot, image, expand):
    return pl.pallas_call(
        edges_kernel,
        in_specs=[SMEM, APART, APART, APART],
        out_specs=[WHOLE] * 2,
        out_shape=[pltpu.VMEM((56, 2048), BF16)] * 2,
        scratch_shapes=[
            pltpu.VMEM((8192, 128), BF16),
            pltpu.VMEM((1, 3, 8, 2048), BF16),
            pltpu.VMEM((64, 256), BF16),
            pltpu.VMEM((1024, 512), BF16),
            pltpu.SemaphoreType.DMA((6,)),
        ],
        compiler_params=params(),
        name="edges",
    )(far(tissue), far(cot), far(image), far(expand))


def main(tissue, *others):
    return pl.pallas_call(
        main_kernel,
        in_specs=[SMEM] + [WHOLE] * 8,
        out_specs=[APART, WHOLE],
        out_shape=[jax.ShapeDtypeStruct((2048, 128), BF16), pltpu.VMEM((512, 128), F32)],
        scratch_shapes=[
            pltpu.VMEM((64, 2048), F32),
            pltpu.VMEM((1024 + 2 * PAD, 128), F32),
            pltpu.VMEM((1024, 512), BF16),
            pltpu.VMEM((1024 + 2 * PAD, 512), F32),
            pltpu.VMEM((1024, 256), F32),
            pltpu.VMEM((1024, 1152), BF16),
            pltpu.VMEM((1024, 256), BF16),
            pltpu.VMEM((1024, 384), BF16),
            pltpu.VMEM((1024 + 2 * PAD, 768), F32),
            pltpu.VMEM((2, 1024, 256), BF16),
            pltpu.VMEM((2048, 128), BF16),
            pltpu.SemaphoreType.DMA((2,)),
        ],
        compiler_params=params(),
        name="main",
    )(far(tissue), *map(near, others))


def unpack(totals):
    return pl.pallas_call(
        unpack_kernel,
        in_specs=[WHOLE],
        out_specs=[WHOLE] * 3,
        out_shape=shapes(((64, 147), F32), ((64, 576), F32), ((64, 256), F32)),
        compiler_params=params(),
        name="unpack",
    )(near(totals))


def reduce_all(totals):
    slide = ("x", "y", "core")
    count, depth = lax.axis_size(slide), lax.axis_size("tile")
    part = lax.all_to_all(totals.reshape(count, -1, 128), slide, 0, 0, tiled=True).sum(0)
    part = lax.all_to_all(jnp.broadcast_to(part[None], (depth,) + part.shape), "tile", 0, 0, tiled=True).sum(0)
    part = part.astype(BF16)
    whole = lax.all_to_all(jnp.broadcast_to(part[None], (count,) + part.shape), slide, 0, 0, tiled=True)
    return whole.reshape(totals.shape)


def per_device(image, stem_weight, conv_weight, expand_weight, cotangent, tissue):
    depth = lax.axis_size("tile")
    rows = tissue[0]
    cot = cotangent[0].reshape(4, 1024, 2, 128).transpose(1, 2, 0, 3).reshape(8192, 128)
    first, second = edges(rows, cot, image, expand_weight)
    pairs = [[(i, i + 1) for i in range(start, depth - 1, 2)] for start in (0, 1)]
    first = lax.ppermute(first, "tile", pairs[0] + [(b, a) for a, b in pairs[0]])
    second = lax.ppermute(second, "tile", pairs[1] + [(b, a) for a, b in pairs[1]])
    cot_f, back2, w1, w2, w2b = prepare(rows, cot, expand_weight, stem_weight.T, conv_weight.T)
    out, totals = main(rows, image, first, second, w1, w2, back2, w2b, cot_f)
    stem_g, conv_g, expand_g = unpack(reduce_all(totals))
    field = out.reshape(512, 4, 128).transpose(1, 0, 2)
    field = with_layout_constraint(field, Layout(major_to_minor=(1, 0, 2)))
    return field.reshape(1, 4, 65536), stem_g.T, conv_g.T, expand_g


def solution(mesh):
    slide = ("x", "y", "core")
    fine = Mesh(mesh.devices.reshape(4, 4, 2, 8), slide + ("tile",))
    placed = (P(slide, None, "tile", None), P(), P(), P(), P(slide, "tile", None), P(slide, None, None))
    return jax.shard_map(
        per_device, mesh=fine, in_specs=placed, out_specs=(P(slide, "tile", None), P(), P(), P()), check_vma=False
    )
```
